512 devices in a mesh: group: 16 (over z_lo, core), resp: 8 (over y, z_hi), vocab: 4 (over x).
Axes of the slice: x: 4, y: 4, z: 16 (z_hi: 2, z_lo: 8; z = z_hi * 8 + z_lo), core: 2. Of those that a mesh axis runs over, the one named last changes fastest.
Arguments:
- queries: bfloat16 [16, 32, 128, 5120], P('group', ('resp', 'vocab')), may hold values from -200 to 200
- own_kv: bfloat16 [16, 32, 128, 2, 640], P('group', ('resp', 'vocab')), may hold values from -6 to 6
- prefix_kv: bfloat16 [16, 128, 2, 640], P('group', ('resp', 'vocab')), may hold values from -20 to 20
- out_grad: bfloat16 [16, 32, 128, 5120], P('group', ('resp', 'vocab')), may hold values from -6 to 6
- lengths: int32 [16, 32], P('group', ('resp', 'vocab')), may hold values from 32 to 128
- advantages: float32 [16, 32], P('group', ('resp', 'vocab')), may hold values from -4 to 4
Outputs:
- query_grad: bfloat16 [16, 32, 128, 5120], P('group', ('resp', 'vocab'))
- own_kv_grad: bfloat16 [16, 32, 128, 2, 640], P('group', ('resp', 'vocab'))
- prefix_kv_grad: float32 [16, 128, 2, 640], P('group', ('resp', 'vocab'))
- token_scale: float32 [], replicated
The draws below stay inside these ranges and needn't reach their ends.
All inputs are finite; a program needn't handle non-finite values.
Results may differ from the reference program's by a relative error of at most 0.039.
Values may be sent and summed in bfloat16 or wider, within the bound.
A program may use at most 64 MiB of HBM per device.

```python
import math
import jax
import jax.numpy as jnp
from jax import lax

DH = 128
KVH = 5
GQA = 8
L = 128
D = 5120
KVW = 640
GROUPS = 16
RESPONSES = 32
PREFIX = 128
SLOTS = 65536


def prefix_parts(key):
    key_keys, key_values, key_scale = jax.random.split(key, 3)
    prefix_keys = jnp.clip(jax.random.normal(key_keys, (GROUPS, PREFIX, KVH * DH), jnp.float32), -6.0, 6.0)
    prefix_values = jnp.clip(jax.random.normal(key_values, (GROUPS, PREFIX, KVH * DH), jnp.float32), -6.0, 6.0)
    column_scale = jnp.exp(jax.random.uniform(key_scale, (KVH * DH,), jnp.float32, jnp.log(0.3), jnp.log(3.3)))
    prefix_values = prefix_values * column_scale
    return (prefix_keys, prefix_values)


def draw_prefix_kv(key, part):
    prefix_keys, prefix_values = prefix_parts(key)
    return jnp.stack([prefix_keys, prefix_values], axis=2).astype(jnp.bfloat16)


def draw_queries(key, part):
    key = jax.random.fold_in(key, 12)
    normals = jnp.clip(jax.random.normal(key, (GROUPS, RESPONSES, L, KVH * GQA * DH), jnp.float32), -6.0, 6.0)
    return normals.astype(jnp.bfloat16)


def draw_lengths(key, part):
    key = jax.random.fold_in(key, 14)
    count = GROUPS * RESPONSES
    order = jnp.arange(count, dtype=jnp.int32)
    base = L // 4 + 3 * L // 4 * order // (count - 1)
    jitter = jax.random.randint(key, (count,), 0, L // 8 + 1, dtype=jnp.int32) * (order > 0).astype(jnp.int32)
    return jnp.minimum(base + jitter, L).reshape(GROUPS, RESPONSES).astype(jnp.int32)


def steps_of(own_key, shape, cuts, low, top_value):
    def one(axis_at, parts):
        steps = jax.random.uniform(jax.random.fold_in(jax.random.fold_in(own_key, 6), axis_at), (parts,), jnp.float32, low / len(cuts), top_value / len(cuts))
        return jnp.repeat(jnp.exp(steps), shape[axis_at] // parts).reshape((-1,) + (1,) * (len(shape) - axis_at - 1))

    level = one(*cuts[0])
    for cut in cuts[1:]:
        level = level * one(*cut)
    return level


def gaussian(stream_key, extent, width, bound, cuts=(), kind=jnp.bfloat16):
    factor_of = steps_of(stream_key, extent, cuts, -0.22, 0.18) if cuts else 1.0
    entries = jax.random.normal(stream_key, extent, jnp.float32) * width * factor_of
    return jnp.minimum(jnp.maximum(entries, -bound), bound).astype(kind)


def setup_inputs(seed: int = 0) -> dict:
    arg_keys = jax.random.split(jax.random.key(seed), 7)
    queries = draw_queries(jax.random.fold_in(arg_keys[6], 71), 0)
    own_kv = gaussian(arg_keys[1], (GROUPS, RESPONSES, L, 2, KVW), 1.0, 6.0, ((0, 16), (1, 32)))
    prefix_kv = draw_prefix_kv(jax.random.fold_in(arg_keys[6], 71), 0)
    out_grad = gaussian(arg_keys[3], (GROUPS, RESPONSES, L, D), 1.0, 6.0, ((0, 16), (1, 32)))
    lengths = draw_lengths(jax.random.fold_in(arg_keys[6], 71), 0)
    advantages = gaussian(arg_keys[5], (GROUPS, RESPONSES), 1.0, 4.0, ((0, 16), (1, 32)), jnp.float32)
    return dict(queries=queries, own_kv=own_kv, prefix_kv=prefix_kv, out_grad=out_grad, lengths=lengths, advantages=advantages)


def response_terms(queries, own_kv, prefix_kv, out_grad, length, advantage, token_scale):
    factor = 1.0 / math.sqrt(DH)
    query = queries.astype(jnp.float32).reshape(L, KVH, GQA, DH)
    pre_keys = prefix_kv[:, 0].astype(jnp.float32).reshape(PREFIX, KVH, DH)
    pre_values = prefix_kv[:, 1].astype(jnp.float32).reshape(PREFIX, KVH, DH)
    own_keys = own_kv[:, 0].astype(jnp.float32).reshape(L, KVH, DH)
    own_values = own_kv[:, 1].astype(jnp.float32).reshape(L, KVH, DH)
    score_pre = jnp.einsum('ikgd,jkd->kgij', query, pre_keys) * factor
    score_own = jnp.einsum('ikgd,jkd->kgij', query, own_keys) * factor
    positions = jnp.arange(L)
    causal = positions[:, None] >= positions[None, :]
    score_own = jnp.where(causal, score_own, -jnp.inf)
    row_peak = jnp.maximum(lax.optimization_barrier(jnp.max(score_pre, axis=3)), lax.optimization_barrier(jnp.max(score_own, axis=3)))
    exp_pre = jnp.exp(score_pre - row_peak[..., None])
    exp_own = jnp.exp(score_own - row_peak[..., None])
    row_total = lax.optimization_barrier(jnp.sum(exp_pre, axis=3)) + lax.optimization_barrier(jnp.sum(exp_own, axis=3))
    prob_pre = exp_pre / row_total[..., None]
    prob_own = exp_own / row_total[..., None]
    weight_pre = prob_pre.astype(jnp.bfloat16).astype(jnp.float32)
    weight_own = prob_own.astype(jnp.bfloat16).astype(jnp.float32)
    mixed = jnp.einsum('kgij,jkd->ikgd', weight_pre, pre_values) + jnp.einsum('kgij,jkd->ikgd', weight_own, own_values)
    attended_f = mixed.astype(jnp.bfloat16).astype(jnp.float32)
    usable = (positions < length).astype(jnp.float32)
    row_weight = usable * advantage * token_scale
    grad_in = (out_grad.astype(jnp.float32) * row_weight[:, None]).astype(jnp.bfloat16)
    grad_f = grad_in.astype(jnp.float32).reshape(L, KVH, GQA, DH)
    row_delta = jnp.einsum('ikgd,ikgd->kgi', grad_f, attended_f)
    dprob_pre = jnp.einsum('ikgd,jkd->kgij', grad_f, pre_values)
    dprob_own = jnp.einsum('ikgd,jkd->kgij', grad_f, own_values)
    dscore_pre = (prob_pre * (dprob_pre - row_delta[..., None])).astype(jnp.bfloat16).astype(jnp.float32)
    dscore_own = (prob_own * (dprob_own - row_delta[..., None])).astype(jnp.bfloat16).astype(jnp.float32)
    query_grad = (jnp.einsum('kgij,jkd->ikgd', dscore_pre, pre_keys) + jnp.einsum('kgij,jkd->ikgd', dscore_own, own_keys)) * factor
    query_grad = query_grad.reshape(L, D).astype(jnp.bfloat16)
    own_grad_k = jnp.einsum('kgij,ikgd->jkd', dscore_own, query) * factor
    own_grad_v = jnp.einsum('kgij,ikgd->jkd', weight_own, grad_f)
    own_grad = jnp.stack([own_grad_k.reshape(L, KVW), own_grad_v.reshape(L, KVW)], axis=1).astype(jnp.bfloat16)
    pre_grad_k = jnp.einsum('kgij,ikgd->jkd', dscore_pre, query) * factor
    pre_grad_v = jnp.einsum('kgij,ikgd->jkd', weight_pre, grad_f)
    prefix_grad = jnp.stack([pre_grad_k.reshape(PREFIX, KVW), pre_grad_v.reshape(PREFIX, KVW)], axis=1)
    return (query_grad, own_grad, prefix_grad)

def reference(queries, own_kv, prefix_kv, out_grad, lengths, advantages):
    valid_total = jnp.sum(lengths)
    token_scale = jnp.float32(SLOTS) / valid_total.astype(jnp.float32)

    def per_group(group_items):
        group_queries, group_own, group_prefix, group_grad, group_lengths, group_adv = group_items

        def per_response(running, items):
            query_grad, own_grad, prefix_grad = response_terms(items[0], items[1], group_prefix, items[2], items[3], items[4], token_scale)
            return (running + prefix_grad, (query_grad, own_grad))
        start = jnp.zeros((PREFIX, 2, KVW), jnp.float32)
        total, (query_grads, own_grads) = lax.scan(per_response, start, (group_queries, group_own, group_grad, group_lengths, group_adv))
        return (query_grads, own_grads, total)
    query_grad, own_kv_grad, prefix_kv_grad = lax.map(per_group, (queries, own_kv, prefix_kv, out_grad, lengths, advantages))
    return (query_grad, own_kv_grad, prefix_kv_grad, token_scale)
```

```python
import math

import jax
import jax.numpy as jnp
from jax import lax
from jax.experimental import pallas as pl
from jax.experimental.pallas import tpu as pltpu
from jax.sharding import PartitionSpec as P

DH = 128
KVH = 5
GQA = 8
TOKENS = 128
WIDTH = GQA * DH
PAIR = 2 * TOKENS
SIDE = 4
PLANE = SIDE * SIDE
FACTOR = 1.0 / math.sqrt(DH)
EXP_SCALE = FACTOR * math.log2(math.e)
LOW = -1e30
MESH = pl.DeviceIdType.MESH
F32 = jnp.float32
BF16 = jnp.bfloat16
LAST = (((1,), (1,)), ((), ()))


def dot_last(a, b):
    return lax.dot_general(a, b, LAST, preferred_element_type=F32)


def dot(a, b):
    return jnp.dot(a, b, preferred_element_type=F32)


def kernel(
    slots,
    len_ref, adv_ref, q_hbm, own_hbm, pre_hbm, do_hbm,
    qg_hbm, own_out, pre_out, scale_out,
    qs, dos, own, pre, own_k, own_v, pre_k, e_own, dp_own, stat, pt, dst, dqt, ogr, qg,
    z_out, z_in, gat, rs_out, rs_in, part, zs_out, zs_in, l_out, l_in,
    in_sem, small_sem, out_sem, z_sem, g_send, g_recv, rs_send, rs_recv, zs_send, zs_recv, l_send, l_recv,
):
    group = lax.axis_index("group")
    resp = lax.axis_index("resp")
    vocab = lax.axis_index("vocab")
    half = resp % 2
    row = resp // 2

    def mate(d, sign):
        there_y = (row + SIDE + sign * (d // SIDE)) % SIDE
        there_x = (vocab + SIDE + sign * (d % SIDE)) % SIDE
        return (group, there_y * 2 + half, there_x)

    opposite = (group, row * 2 + 1 - half, vocab)

    def other_group(stage):
        step = 2**stage
        bit = (group // step) % 2
        return (group + step - 2 * step * bit, resp, vocab)

    barrier = pltpu.get_barrier_semaphore()

    def greet(d, carry):
        pl.semaphore_signal(barrier, inc=1, device_id=mate(d, 1), device_id_type=MESH)
        return carry

    pl.semaphore_signal(barrier, inc=1, device_id=opposite, device_id_type=MESH)
    lax.fori_loop(1, PLANE, greet, 0)
    for stage in range(4):
        pl.semaphore_signal(barrier, inc=1, device_id=other_group(stage), device_id_type=MESH)

    pre_copy = pltpu.make_async_copy(pre_hbm, pre, small_sem.at[0])
    own_copy = pltpu.make_async_copy(own_hbm, own, small_sem.at[1])
    pre_copy.start()
    own_copy.start()

    def in_copies(k):
        cols = pl.ds(pl.multiple_of(k * WIDTH, WIDTH), WIDTH)
        return (
            pltpu.make_async_copy(q_hbm.at[:, cols], qs.at[k], in_sem.at[0, k]),
            pltpu.make_async_copy(do_hbm.at[:, cols], dos.at[k], in_sem.at[1, k]),
        )

    for k in range(KVH):
        for copy in in_copies(k):
            copy.start()

    tile_rows = lax.broadcasted_iota(jnp.int32, (16, DH), 0)
    length = len_ref[0, 0]
    z_out[0] = jnp.where(tile_rows // 4 == half, length.astype(F32), 0.0).astype(BF16)
    pre_copy.wait()
    shard = pre[...].astype(F32)
    blank = jnp.zeros((4, DH), F32)
    for k in range(KVH):
        cols = slice(k * DH, (k + 1) * DH)
        keys = shard[:, 0, cols]
        values = shard[:, 1, cols]
        low = jnp.concatenate([keys, blank, values, blank], axis=0)
        high = jnp.concatenate([blank, keys, blank, values], axis=0)
        z_out[k + 1] = jnp.where(half == 0, low, high).astype(BF16)

    pl.semaphore_wait(barrier, PLANE + 4)
    z_copy = pltpu.make_async_remote_copy(
        src_ref=z_out, dst_ref=z_in, send_sem=z_sem.at[0], recv_sem=z_sem.at[1],
        device_id=opposite, device_id_type=MESH,
    )
    z_copy.start()

    own_copy.wait()
    own_rows = own[...]
    own_keys = own_rows[:, 0, :]
    own_values = own_rows[:, 1, :]
    for k in range(KVH):
        own_k[k] = own_keys[:, k * DH : (k + 1) * DH]
        own_v[k] = own_values[:, k * DH : (k + 1) * DH]

    lane = lax.broadcasted_iota(jnp.int32, (1, PAIR), 1) % TOKENS
    weight = jnp.where(lane < length, adv_ref[0, 0], 0.0)
    key_at = lax.broadcasted_iota(jnp.int32, (TOKENS, PAIR), 0)
    query_at = lax.broadcasted_iota(jnp.int32, (TOKENS, PAIR), 1) % TOKENS
    causal = key_at <= query_at

    def pair_of(ref, k, c):
        return jnp.concatenate(
            [ref[k, :, (2 * c) * DH : (2 * c + 1) * DH], ref[k, :, (2 * c + 1) * DH : (2 * c + 2) * DH]], axis=0
        )

    def all_of(ref, k):
        return jnp.concatenate([ref[k, :, g * DH : (g + 1) * DH] for g in range(GQA)], axis=0)

    def own_part(k, carry):
        for copy in in_copies(k):
            copy.wait()
        keys = own_k[k]
        values = own_v[k]
        for c in range(GQA // 2):
            cols = slice(c * PAIR, (c + 1) * PAIR)
            score = jnp.where(causal, dot_last(keys, pair_of(qs, k, c)), LOW)
            peak = jnp.max(score, axis=0, keepdims=True)
            e = jnp.exp2((score - peak) * EXP_SCALE)
            dprob = dot_last(values, pair_of(dos, k, c))
            e_own[k, :, cols] = e
            dp_own[k, :, cols] = dprob
            stat[k, 0:1, cols] = peak
            stat[k, 1:2, cols] = jnp.sum(e, axis=0, keepdims=True)
            stat[k, 2:3, cols] = jnp.sum(e * dprob, axis=0, keepdims=True)
        return carry

    lax.fori_loop(0, 2, own_part, 0)

    z_copy.wait_recv()
    gat[0] = (z_out[...].astype(F32) + z_in[...].astype(F32)).astype(BF16)
    parts = ((0, 2), (2, 4))

    def spread(part_at):
        start, count = parts[part_at]

        def send(d, carry):
            pltpu.make_async_remote_copy(
                src_ref=gat.at[0, pl.ds(start, count)], dst_ref=gat.at[d, pl.ds(start, count)],
                send_sem=g_send.at[part_at], recv_sem=g_recv.at[part_at],
                device_id=mate(d, 1), device_id_type=MESH,
            ).start()
            return carry

        lax.fori_loop(1, PLANE, send, 0)

    def spread_all(part_at):
        start, count = parts[part_at]
        block = gat.at[pl.ds(1, PLANE - 1), pl.ds(start, count)]
        return pltpu.make_async_remote_copy(
            src_ref=block, dst_ref=block, send_sem=g_send.at[part_at], recv_sem=g_recv.at[part_at],
            device_id=opposite, device_id_type=MESH,
        )

    spread(0)
    spread(1)
    lax.fori_loop(2, KVH, own_part, 0)

    def length_copy(stage):
        return pltpu.make_async_remote_copy(
            src_ref=l_out.at[stage], dst_ref=l_in.at[stage], send_sem=l_send.at[stage], recv_sem=l_recv.at[stage],
            device_id=other_group(stage), device_id_type=MESH,
        )

    def length_step(stage):
        length_copy(stage).wait_recv()
        l_out[stage + 1] = l_out[stage] + l_in[stage]
        if stage < 3:
            length_copy(stage + 1).start()

    spread_all(0).wait_recv()
    counts = jnp.sum(gat[:, 0].astype(F32), axis=0)
    l_out[0] = jnp.broadcast_to(jnp.sum(counts, axis=0, keepdims=True) * 0.25, (8, DH))
    length_copy(0).start()

    def scatter(k):
        def send(d, carry):
            pltpu.make_async_remote_copy(
                src_ref=rs_out.at[k, d], dst_ref=rs_in.at[k, d], send_sem=rs_send.at[k], recv_sem=rs_recv.at[k],
                device_id=mate(d, -1), device_id_type=MESH,
            ).start()
            return carry

        lax.fori_loop(1, PLANE, send, 0)

    def scatter_all(k):
        return pltpu.make_async_remote_copy(
            src_ref=rs_out.at[k, pl.ds(1, PLANE - 1)], dst_ref=rs_in.at[k, pl.ds(1, PLANE - 1)],
            send_sem=rs_send.at[k], recv_sem=rs_recv.at[k], device_id=opposite, device_id_type=MESH,
        )

    def cross(k):
        return pltpu.make_async_remote_copy(
            src_ref=zs_out.at[k], dst_ref=zs_in.at[k], send_sem=zs_send.at[k], recv_sem=zs_recv.at[k],
            device_id=opposite, device_id_type=MESH,
        )

    def plane_sum(k):
        scatter_all(k).wait_recv()
        total = part[k] + jnp.sum(rs_in[k, 1:PLANE].astype(F32), axis=0)
        part[k] = total
        zs_out[k] = total.astype(BF16)
        cross(k).start()

    def prefix_part(k, carry):
        @pl.when(k == 1)
        def _():
            spread_all(1).wait_recv()

        tile = gat[:, k + 1].astype(F32)
        keys = tile[:, 0:8, :].reshape(TOKENS, DH).astype(BF16)
        values = tile[:, 8:16, :].reshape(TOKENS, DH).astype(BF16)
        pre_k[k] = keys
        for c in range(GQA // 2):
            cols = slice(c * PAIR, (c + 1) * PAIR)
            score = dot_last(keys, pair_of(qs, k, c))
            own_peak = stat[k, 0:1, cols]
            peak = jnp.maximum(own_peak, jnp.max(score, axis=0, keepdims=True))
            e = jnp.exp2((score - peak) * EXP_SCALE)
            dprob = dot_last(values, pair_of(dos, k, c))
            shrink = jnp.exp2((own_peak - peak) * EXP_SCALE)
            inverse = 1.0 / (jnp.sum(e, axis=0, keepdims=True) + shrink * stat[k, 1:2, cols])
            delta = (jnp.sum(e * dprob, axis=0, keepdims=True) + shrink * stat[k, 2:3, cols]) * inverse
            scaled = inverse * weight
            prob = e * scaled
            pt[:, cols] = prob.astype(BF16)
            dst[k, 0:TOKENS, cols] = (prob * (dprob - delta)).astype(BF16)
            stat[k, 3:4, cols] = shrink * scaled
            stat[k, 4:5, cols] = delta
        grad_k = dot(dst[k, 0:TOKENS, :], all_of(qs, k)) * FACTOR
        grad_v = dot(pt[...], all_of(dos, k))
        both = jnp.concatenate([grad_k.reshape(PLANE, 8, DH), grad_v.reshape(PLANE, 8, DH)], axis=1)
        part[k] = both[0]
        rs_out[k] = both.astype(BF16)
        scatter(k)

        @pl.when(k >= 2)
        def _():
            plane_sum(k - 2)

        @pl.when(k == 2)
        def _():
            length_step(0)

        return carry

    lax.fori_loop(0, KVH, prefix_part, 0)
    length_step(1)

    def own_grads(k):
        for c in range(GQA // 2):
            cols = slice(c * PAIR, (c + 1) * PAIR)
            prob = e_own[k, :, cols] * stat[k, 3:4, cols]
            pt[:, cols] = prob.astype(BF16)
            dst[k, TOKENS:PAIR, cols] = (prob * (dp_own[k, :, cols] - stat[k, 4:5, cols])).astype(BF16)
        ogr[k, 0] = dot(dst[k, TOKENS:PAIR, :], all_of(qs, k)) * FACTOR
        ogr[k, 1] = dot(pt[...], all_of(dos, k))
        keys = jnp.concatenate([pre_k[k].astype(F32).T, own_k[k].astype(F32).T], axis=1).astype(BF16)
        dqt[k] = dot(keys, dst[k]) * FACTOR

    def first_heads(k, carry):
        own_grads(k)
        plane_sum(k + 3)
        return carry

    def last_heads(k, carry):
        own_grads(k)
        return carry

    lax.fori_loop(0, 2, first_heads, 0)
    length_step(2)
    lax.fori_loop(2, KVH, last_heads, 0)
    length_step(3)
    scale = slots / l_out[4]
    scale_out[...] = scale[0:1, 0:1]
    one = scale[0:1, :]

    def out_copy(k):
        cols = pl.ds(pl.multiple_of(k * WIDTH, WIDTH), WIDTH)
        return pltpu.make_async_copy(qg.at[k], qg_hbm.at[:, cols], out_sem.at[k])

    def finish(k, carry):
        for g in range(GQA):
            cols = slice(g * DH, (g + 1) * DH)
            qg[k, :, cols] = (dqt[k, :, cols].T * one).astype(BF16)
        out_copy(k).start()
        return carry

    lax.fori_loop(0, KVH, finish, 0)
    for k in range(KVH):
        cols = slice(k * DH, (k + 1) * DH)
        own_out[0, :, cols] = (ogr[k, 0] * one).astype(BF16)
        own_out[1, :, cols] = (ogr[k, 1] * one).astype(BF16)

    for k in range(KVH):
        cols = slice(k * DH, (k + 1) * DH)
        cross(k).wait_recv()
        total = (part[k] + zs_in[k].astype(F32)) * one
        pre_out[:, 0, cols] = jnp.where(half == 0, total[0:4], total[4:8])
        pre_out[:, 1, cols] = jnp.where(half == 0, total[8:12], total[12:16])

    for k in range(KVH):
        out_copy(k).wait()
        scatter_all(k).wait_send()
        cross(k).wait_send()
    for stage in range(4):
        length_copy(stage).wait_send()
    spread_all(0).wait_send()
    spread_all(1).wait_send()
    z_copy.wait_send()


def on_device(queries, own_kv, prefix_kv, out_grad, lengths, advantages):
    slots = float(
        queries.shape[2] * lax.axis_size("group") * lax.axis_size("resp") * lax.axis_size("vocab")
    )
    width = KVH * WIDTH
    vmem = pltpu.VMEM
    dma = pltpu.SemaphoreType.DMA
    anywhere = pl.BlockSpec(memory_space=pl.ANY)
    in_smem = pl.BlockSpec(memory_space=pltpu.SMEM)
    in_vmem = pl.BlockSpec(memory_space=pltpu.VMEM)

    def body(*refs):
        kernel(slots, *refs)

    query_grad, own_grad, prefix_grad, token_scale = pl.pallas_call(
        body,
        out_shape=(
            jax.ShapeDtypeStruct((TOKENS, width), BF16),
            jax.ShapeDtypeStruct((2, TOKENS, KVH * DH), BF16),
            jax.ShapeDtypeStruct((4, 2, KVH * DH), F32),
            jax.ShapeDtypeStruct((1, 1), F32),
        ),
        in_specs=[in_smem, in_smem, anywhere, anywhere, anywhere, anywhere],
        out_specs=(anywhere, in_vmem, in_vmem, in_vmem),
        scratch_shapes=[
            vmem((KVH, TOKENS, WIDTH), BF16),
            vmem((KVH, TOKENS, WIDTH), BF16),
            vmem((TOKENS, 2, KVH * DH), BF16),
            vmem((4, 2, KVH * DH), BF16),
            vmem((KVH, TOKENS, DH), BF16),
            vmem((KVH, TOKENS, DH), BF16),
            vmem((KVH, TOKENS, DH), BF16),
            vmem((KVH, TOKENS, WIDTH), F32),
            vmem((KVH, TOKENS, WIDTH), F32),
            vmem((KVH, 8, WIDTH), F32),
            vmem((TOKENS, WIDTH), BF16),
            vmem((KVH, PAIR, WIDTH), BF16),
            vmem((KVH, DH, WIDTH), F32),
            vmem((KVH, 2, TOKENS, DH), F32),
            vmem((KVH, TOKENS, WIDTH), BF16),
            vmem((KVH + 1, 16, DH), BF16),
            vmem((KVH + 1, 16, DH), BF16),
            vmem((PLANE, KVH + 1, 16, DH), BF16),
            vmem((KVH, PLANE, 16, DH), BF16),
            vmem((KVH, PLANE, 16, DH), BF16),
            vmem((KVH, 16, DH), F32),
            vmem((KVH, 16, DH), BF16),
            vmem((KVH, 16, DH), BF16),
            vmem((5, 8, DH), F32),
            vmem((4, 8, DH), F32),
            dma((2, KVH)),
            dma((2,)),
            dma((KVH,)),
            dma((2,)),
            dma((2,)),
            dma((2,)),
            dma((KVH,)),
            dma((KVH,)),
            dma((KVH,)),
            dma((KVH,)),
            dma((4,)),
            dma((4,)),
        ],
        compiler_params=pltpu.CompilerParams(
            collective_id=0, has_side_effects=True, vmem_limit_bytes=48 * 1024 * 1024
        ),
        cost_estimate=pl.CostEstimate(
            flops=5 * KVH * 2 * WIDTH * PAIR * DH,
            bytes_accessed=5 * 1024 * 1024,
            transcendentals=KVH * WIDTH * PAIR,
        ),
    )(lengths, advantages, queries[0, 0], own_kv[0, 0], prefix_kv[0], out_grad[0, 0])
    own_grad = jnp.swapaxes(own_grad, 0, 1)
    return query_grad[None, None], own_grad[None, None], prefix_grad[None], token_scale[0, 0]


def solution(mesh):
    in_specs = (
        P("group", ("resp", "vocab"), None, None),
        P("group", ("resp", "vocab"), None, None, None),
        P("group", ("resp", "vocab"), None, None),
        P("group", ("resp", "vocab"), None, None),
        P("group", ("resp", "vocab")),
        P("group", ("resp", "vocab")),
    )
    out_specs = (
        P("group", ("resp", "vocab"), None, None),
        P("group", ("resp", "vocab"), None, None, None),
        P("group", ("resp", "vocab"), None, None),
        P(),
    )
    return jax.shard_map(
        on_device, mesh=mesh, in_specs=in_specs, out_specs=out_specs, check_vma=False
    )
```

```python
import math

import jax
import jax.numpy as jnp
from jax import lax
from jax.experimental import pallas as pl
from jax.experimental.pallas import tpu as pltpu
from jax.sharding import PartitionSpec as P

DH = 128
KVH = 5
GQA = 8
TOKENS = 128
WIDTH = GQA * DH
PAIR = 2 * TOKENS
SIDE = 4
PLANE = SIDE * SIDE
FACTOR = 1.0 / math.sqrt(DH)
EXP_SCALE = FACTOR * math.log2(math.e)
LOW = -1e30
MESH = pl.DeviceIdType.MESH
F32 = jnp.float32
BF16 = jnp.bfloat16
LAST = (((1,), (1,)), ((), ()))


def dot_last(a, b):
    return lax.dot_general(a, b, LAST, preferred_element_type=F32)


def dot(a, b):
    return jnp.dot(a, b, preferred_element_type=F32)


def kernel(
    slots,
    len_ref, adv_ref, q_hbm, own_hbm, pre_hbm, do_hbm,
    qg, own_out, pre_out, scale_out,
    qs, dos, own, pre, own_k, own_v, pre_k, e_own, dp_own, stat, pt, dst, ogr, own_t,
    z_out, z_in, gat, rs_out, rs_in, part, zs_out, zs_in, l_out, la_in, lb_in, lp_in, lz_in,
    in_sem, small_sem, z_send, z_recv, g_send, g_recv, rs_send, rs_recv, zs_send, zs_recv, l_send, l_recv,
):
    group = lax.axis_index("group")
    resp = lax.axis_index("resp")
    vocab = lax.axis_index("vocab")
    half = resp % 2
    row = resp // 2

    ahead, behind = [None], [None]
    for d in range(1, PLANE):
        down, over = d // SIDE, d % SIDE
        ahead.append((group, ((row + down) % SIDE) * 2 + half, (vocab + over) % SIDE))
        behind.append((group, ((row + SIDE - down) % SIDE) * 2 + half, (vocab + SIDE - over) % SIDE))
    opposite = (group, row * 2 + 1 - half, vocab)
    near = [None] + [((group // 4) * 4 + (group + o) % 4, resp, vocab) for o in range(1, 4)]
    far = [None] + [((group + 4 * o) % 16, resp, vocab) for o in range(1, 4)]

    barrier = pltpu.get_barrier_semaphore()
    partners = [opposite] + ahead[1:] + near[1:] + far[1:]
    for partner in partners:
        pl.semaphore_signal(barrier, inc=1, device_id=partner, device_id_type=MESH)

    pre_copy = pltpu.make_async_copy(pre_hbm, pre, small_sem.at[0])
    own_copy = pltpu.make_async_copy(own_hbm, own, small_sem.at[1])
    pre_copy.start()
    own_copy.start()

    def in_copies(k):
        cols = pl.ds(pl.multiple_of(k * WIDTH, WIDTH), WIDTH)
        return (
            pltpu.make_async_copy(q_hbm.at[:, cols], qs.at[k], in_sem.at[0, k]),
            pltpu.make_async_copy(do_hbm.at[:, cols], dos.at[k], in_sem.at[1, k]),
        )

    for k in range(KVH):
        for copy in in_copies(k):
            copy.start()

    length = len_ref[0, 0]
    l_out[0] = jnp.full((8, DH), length.astype(F32))
    blank = jnp.zeros((8, DH), F32)
    pre_copy.wait()
    shard = pre[...].astype(F32)
    mine = []
    for k in range(KVH):
        cols = slice(k * DH, (k + 1) * DH)
        mine.append(jnp.concatenate([shard[:, 0, cols], shard[:, 1, cols]], axis=0))
    for t in range(3):
        low = mine[2 * t]
        high = mine[2 * t + 1] if 2 * t + 1 < KVH else blank
        z_out[t] = jnp.concatenate([low, high], axis=0).astype(BF16)

    def z_copy(at):
        tiles = pl.ds(0, 1) if at == 0 else pl.ds(1, 2)
        return pltpu.make_async_remote_copy(
            src_ref=z_out.at[tiles], dst_ref=z_in.at[tiles], send_sem=z_send.at[at], recv_sem=z_recv.at[at],
            device_id=opposite, device_id_type=MESH,
        )

    def send(src, dst, sems, at, to):
        pltpu.make_async_remote_copy(
            src_ref=src, dst_ref=dst, send_sem=sems[0].at[at], recv_sem=sems[1].at[at],
            device_id=to, device_id_type=MESH,
        ).start()

    def landed(block, sems, at):
        return pltpu.make_async_remote_copy(
            src_ref=block, dst_ref=block, send_sem=sems[0].at[at], recv_sem=sems[1].at[at],
            device_id=opposite, device_id_type=MESH,
        )

    g_sems, l_sems, rs_sems = (g_send, g_recv), (l_send, l_recv), (rs_send, rs_recv)

    pl.semaphore_wait(barrier, len(partners))
    z_copy(0).start()
    z_copy(1).start()
    for o in range(1, 4):
        send(l_out.at[0], la_in.at[o], l_sems, 0, near[o])

    own_copy.wait()
    own_rows = own[...]
    own_keys = own_rows[:, 0, :]
    own_values = own_rows[:, 1, :]
    for k in range(KVH):
        own_k[k] = own_keys[:, k * DH : (k + 1) * DH]
        own_v[k] = own_values[:, k * DH : (k + 1) * DH]

    lane = lax.broadcasted_iota(jnp.int32, (1, PAIR), 1) % TOKENS
    weight = jnp.where(lane < length, adv_ref[0, 0], 0.0)
    key_at = lax.broadcasted_iota(jnp.int32, (TOKENS, PAIR), 0)
    query_at = lax.broadcasted_iota(jnp.int32, (TOKENS, PAIR), 1) % TOKENS
    causal = key_at <= query_at

    def pair_of(ref, k, c):
        return jnp.concatenate(
            [ref[k, :, (2 * c) * DH : (2 * c + 1) * DH], ref[k, :, (2 * c + 1) * DH : (2 * c + 2) * DH]], axis=0
        )

    def all_of(ref, k):
        return jnp.concatenate([ref[k, :, g * DH : (g + 1) * DH] for g in range(GQA)], axis=0)

    def own_part(k):
        for copy in in_copies(k):
            copy.wait()
        keys = own_k[k]
        values = own_v[k]
        for c in range(GQA // 2):
            cols = slice(c * PAIR, (c + 1) * PAIR)
            score = jnp.where(causal, dot_last(keys, pair_of(qs, k, c)), LOW)
            peak = jnp.max(score, axis=0, keepdims=True)
            e = jnp.exp2((score - peak) * EXP_SCALE)
            dprob = dot_last(values, pair_of(dos, k, c))
            e_own[k, :, cols] = e
            dp_own[k, :, cols] = dprob
            stat[k, 0:1, cols] = peak
            stat[k, 1:2, cols] = jnp.sum(e, axis=0, keepdims=True)
            stat[k, 2:3, cols] = jnp.sum(e * dprob, axis=0, keepdims=True)

    def own_parts(start, stop):
        def step(k, carry):
            own_part(k)
            return carry

        lax.fori_loop(start, stop, step, 0)

    def unit(k):
        at, rows = k // 2, slice(8 * (k % 2), 8 * (k % 2) + 8)
        here = z_out[at].astype(F32)[rows]
        there = z_in[at].astype(F32)[rows]
        first = jnp.where(half == 0, here, there)
        second = jnp.where(half == 0, there, here)
        gat[0, k] = jnp.concatenate([first[0:4], second[0:4], first[4:8], second[4:8]], axis=0).astype(BF16)

    parts = ((0, 1), (1, 1), (2, 3))

    def spread(at):
        start, count = parts[at]
        for d in range(1, PLANE):
            send(gat.at[0, pl.ds(start, count)], gat.at[d, pl.ds(start, count)], g_sems, at, ahead[d])

    def spread_all(at):
        start, count = parts[at]
        return landed(gat.at[pl.ds(1, PLANE - 1), pl.ds(start, count)], g_sems, at)

    own_part(0)
    landed(la_in.at[pl.ds(1, 3)], l_sems, 0).wait_recv()
    l_out[1] = l_out[0] + la_in[1] + la_in[2] + la_in[3]
    for o in range(1, 4):
        send(l_out.at[1], lb_in.at[o], l_sems, 1, far[o])
    own_parts(1, 3)
    z_copy(0).wait_recv()
    unit(0)
    spread(0)
    unit(1)
    spread(1)
    z_copy(1).wait_recv()
    for k in range(2, KVH):
        unit(k)
    spread(2)
    landed(lb_in.at[pl.ds(1, 3)], l_sems, 1).wait_recv()
    l_out[2] = l_out[1] + lb_in[1] + lb_in[2] + lb_in[3]
    for d in range(1, PLANE):
        send(l_out.at[2], lp_in.at[d], l_sems, 2, ahead[d])
    own_parts(3, KVH)

    def scatter_all(k):
        return landed(rs_out.at[k, pl.ds(1, PLANE - 1)], rs_sems, k)

    def cross(k):
        return pltpu.make_async_remote_copy(
            src_ref=zs_out.at[k], dst_ref=zs_in.at[k], send_sem=zs_send.at[k], recv_sem=zs_recv.at[k],
            device_id=opposite, device_id_type=MESH,
        )

    def plane_sum(k):
        landed(rs_in.at[k, pl.ds(1, PLANE - 1)], rs_sems, k).wait_recv()
        total = part[k] + jnp.sum(rs_in[k, 1:PLANE].astype(F32), axis=0)
        part[k] = total
        zs_out[k] = total.astype(BF16)
        cross(k).start()

    length_cross = pltpu.make_async_remote_copy(
        src_ref=l_out.at[3], dst_ref=lz_in, send_sem=l_send.at[3], recv_sem=l_recv.at[3],
        device_id=opposite, device_id_type=MESH,
    )

    def prefix_part(k, carry):
        @pl.when(k == 0)
        def _():
            spread_all(0).wait_recv()

        @pl.when(k == 1)
        def _():
            spread_all(1).wait_recv()

        @pl.when(k == 2)
        def _():
            spread_all(2).wait_recv()

        tile = gat[:, k].astype(F32)
        keys = tile[:, 0:8, :].reshape(TOKENS, DH).astype(BF16)
        values = tile[:, 8:16, :].reshape(TOKENS, DH).astype(BF16)
        pre_k[k] = keys
        for c in range(GQA // 2):
            cols = slice(c * PAIR, (c + 1) * PAIR)
            score = dot_last(keys, pair_of(qs, k, c))
            own_peak = stat[k, 0:1, cols]
            peak = jnp.maximum(own_peak, jnp.max(score, axis=0, keepdims=True))
            e = jnp.exp2((score - peak) * EXP_SCALE)
            dprob = dot_last(values, pair_of(dos, k, c))
            shrink = jnp.exp2((own_peak - peak) * EXP_SCALE)
            inverse = 1.0 / (jnp.sum(e, axis=0, keepdims=True) + shrink * stat[k, 1:2, cols])
            delta = (jnp.sum(e * dprob, axis=0, keepdims=True) + shrink * stat[k, 2:3, cols]) * inverse
            scaled = inverse * weight
            prob = e * scaled
            pt[:, cols] = prob.astype(BF16)
            dst[k, 0:TOKENS, cols] = (prob * (dprob - delta)).astype(BF16)
            stat[k, 3:4, cols] = shrink * scaled
            stat[k, 4:5, cols] = delta
        grad_k = dot(dst[k, 0:TOKENS, :], all_of(qs, k)) * FACTOR
        grad_v = dot(pt[...], all_of(dos, k))
        both = jnp.concatenate([grad_k.reshape(PLANE, 8, DH), grad_v.reshape(PLANE, 8, DH)], axis=1)
        part[k] = both[0]
        rs_out[k] = both.astype(BF16)
        for d in range(1, PLANE):
            send(rs_out.at[k, d], rs_in.at[k, d], rs_sems, k, behind[d])

        @pl.when(k >= 2)
        def _():
            plane_sum(k - 2)

        @pl.when(k == 1)
        def _():
            landed(lp_in.at[pl.ds(1, PLANE - 1)], l_sems, 2).wait_recv()
            l_out[3] = l_out[2] + jnp.sum(lp_in[1:PLANE], axis=0)
            length_cross.start()

        return carry

    lax.fori_loop(0, KVH, prefix_part, 0)

    def own_grads(k):
        for c in range(GQA // 2):
            cols = slice(c * PAIR, (c + 1) * PAIR)
            prob = e_own[k, :, cols] * stat[k, 3:4, cols]
            pt[:, cols] = prob.astype(BF16)
            dst[k, TOKENS:PAIR, cols] = (prob * (dp_own[k, :, cols] - stat[k, 4:5, cols])).astype(BF16)
        ogr[k, 0] = dot(dst[k, TOKENS:PAIR, :], all_of(qs, k)) * FACTOR
        ogr[k, 1] = dot(pt[...], all_of(dos, k))

    def own_grads_step(k, carry):
        own_grads(k)
        return carry

    own_grads(0)
    plane_sum(3)
    own_grads(1)
    plane_sum(4)
    lax.fori_loop(2, KVH, own_grads_step, 0)
    length_cross.wait_recv()
    scale = slots / (l_out[3] + lz_in[...])
    scale_out[...] = scale[0:1, 0:1]
    one = scale[0:1, :]
    one_k = one * FACTOR

    def query_grads(k, carry):
        head = pl.ds(pl.multiple_of(k * DH, DH), DH)
        own_t[0, :, head] = (ogr[k, 0] * one).astype(BF16)
        own_t[1, :, head] = (ogr[k, 1] * one).astype(BF16)
        keys = jnp.concatenate([pre_k[k].astype(F32).T, own_k[k].astype(F32).T], axis=1).astype(BF16)
        for c in range(GQA // 2):
            turned = dot(keys, dst[k, :, c * PAIR : (c + 1) * PAIR])
            for g in range(2):
                at = pl.ds(pl.multiple_of(k * WIDTH + (2 * c + g) * DH, DH), DH)
                qg[:, at] = (turned[:, g * DH : (g + 1) * DH].T * one_k).astype(BF16)
        return carry

    lax.fori_loop(0, KVH, query_grads, 0)
    own_out[:, 0, :] = own_t[0]
    own_out[:, 1, :] = own_t[1]

    for k in range(KVH):
        cols = slice(k * DH, (k + 1) * DH)
        cross(k).wait_recv()
        total = (part[k] + zs_in[k].astype(F32)) * one
        pre_out[:, 0, cols] = jnp.where(half == 0, total[0:4], total[4:8])
        pre_out[:, 1, cols] = jnp.where(half == 0, total[8:12], total[12:16])

    for k in range(KVH):
        scatter_all(k).wait_send()
        cross(k).wait_send()
    for at in range(3):
        spread_all(at).wait_send()
    for at in range(2):
        z_copy(at).wait_send()
        landed(la_in.at[pl.ds(1, 3)], l_sems, at).wait_send()
    landed(lp_in.at[pl.ds(1, PLANE - 1)], l_sems, 2).wait_send()
    length_cross.wait_send()


def write_out(qg, own, pre, qg_out, own_out, pre_out, sems):
    copies = [pltpu.make_async_copy(pre, pre_out, sems.at[0])]
    for at in range(8):
        rows = pl.ds(16 * at, 16)
        copies.append(pltpu.make_async_copy(qg.at[rows], qg_out.at[rows], sems.at[1 + at]))
    for at in range(2):
        rows = pl.ds(64 * at, 64)
        copies.append(pltpu.make_async_copy(own.at[rows], own_out.at[rows], sems.at[9 + at]))
    for copy in copies:
        copy.start()
    for copy in copies:
        copy.wait()


def on_device(queries, own_kv, prefix_kv, out_grad, lengths, advantages):
    slots = float(
        queries.shape[2] * lax.axis_size("group") * lax.axis_size("resp") * lax.axis_size("vocab")
    )
    width = KVH * WIDTH
    vmem = pltpu.VMEM
    dma = pltpu.SemaphoreType.DMA
    in_hbm = pl.BlockSpec(memory_space=pltpu.HBM)
    in_smem = pl.BlockSpec(memory_space=pltpu.SMEM)
    in_vmem = pl.BlockSpec(memory_space=pltpu.VMEM)

    def body(*refs):
        kernel(slots, *refs)

    def held(x):
        return pltpu.with_memory_space_constraint(x, pltpu.HBM)

    query_shape, own_shape, prefix_shape = (TOKENS, width), (TOKENS, 2, KVH * DH), (4, 2, KVH * DH)
    query_grad, own_grad, prefix_grad, token_scale = pl.pallas_call(
        body,
        out_shape=(
            vmem(query_shape, BF16),
            vmem(own_shape, BF16),
            vmem(prefix_shape, F32),
            jax.ShapeDtypeStruct((1, 1), F32),
        ),
        in_specs=[in_smem, in_smem, in_hbm, in_hbm, in_hbm, in_hbm],
        out_specs=(in_vmem, in_vmem, in_vmem, in_vmem),
        scratch_shapes=[
            vmem((KVH, TOKENS, WIDTH), BF16),
            vmem((KVH, TOKENS, WIDTH), BF16),
            vmem((TOKENS, 2, KVH * DH), BF16),
            vmem((4, 2, KVH * DH), BF16),
            vmem((KVH, TOKENS, DH), BF16),
            vmem((KVH, TOKENS, DH), BF16),
            vmem((KVH, TOKENS, DH), BF16),
            vmem((KVH, TOKENS, WIDTH), F32),
            vmem((KVH, TOKENS, WIDTH), F32),
            vmem((KVH, 8, WIDTH), F32),
            vmem((TOKENS, WIDTH), BF16),
            vmem((KVH, PAIR, WIDTH), BF16),
            vmem((KVH, 2, TOKENS, DH), F32),
            vmem((2, TOKENS, KVH * DH), BF16),
            vmem((3, 16, DH), BF16),
            vmem((3, 16, DH), BF16),
            vmem((PLANE, KVH, 16, DH), BF16),
            vmem((KVH, PLANE, 16, DH), BF16),
            vmem((KVH, PLANE, 16, DH), BF16),
            vmem((KVH, 16, DH), F32),
            vmem((KVH, 16, DH), BF16),
            vmem((KVH, 16, DH), BF16),
            vmem((4, 8, DH), F32),
            vmem((4, 8, DH), F32),
            vmem((4, 8, DH), F32),
            vmem((PLANE, 8, DH), F32),
            vmem((8, DH), F32),
            dma((2, KVH)),
            dma((2,)),
            dma((2,)),
            dma((2,)),
            dma((3,)),
            dma((3,)),
            dma((KVH,)),
            dma((KVH,)),
            dma((KVH,)),
            dma((KVH,)),
            dma((4,)),
            dma((4,)),
        ],
        compiler_params=pltpu.CompilerParams(
            collective_id=0, has_side_effects=True, vmem_limit_bytes=48 * 1024 * 1024
        ),
        cost_estimate=pl.CostEstimate(
            flops=5 * KVH * 2 * WIDTH * PAIR * DH,
            bytes_accessed=5 * 1024 * 1024,
            transcendentals=KVH * WIDTH * PAIR,
        ),
    )(lengths, advantages, held(queries[0, 0]), held(own_kv[0, 0]), held(prefix_kv[0]), held(out_grad[0, 0]))
    query_grad, own_grad, prefix_grad = pl.pallas_call(
        write_out,
        out_shape=(
            jax.ShapeDtypeStruct(query_shape, BF16),
            jax.ShapeDtypeStruct(own_shape, BF16),
            jax.ShapeDtypeStruct(prefix_shape, F32),
        ),
        in_specs=[in_vmem] * 3,
        out_specs=(in_hbm,) * 3,
        scratch_shapes=[dma((11,))],
        compiler_params=pltpu.CompilerParams(vmem_limit_bytes=8 * 1024 * 1024),
    )(query_grad, own_grad, prefix_grad)
    return query_grad[None, None], own_grad[None, None], prefix_grad[None], token_scale[0, 0]


def solution(mesh):
    in_specs = (
        P("group", ("resp", "vocab"), None, None),
        P("group", ("resp", "vocab"), None, None, None),
        P("group", ("resp", "vocab"), None, None),
        P("group", ("resp", "vocab"), None, None),
        P("group", ("resp", "vocab")),
        P("group", ("resp", "vocab")),
    )
    out_specs = (
        P("group", ("resp", "vocab"), None, None),
        P("group", ("resp", "vocab"), None, None, None),
        P("group", ("resp", "vocab"), None, None),
        P(),
    )
    return jax.shard_map(
        on_device, mesh=mesh, in_specs=in_specs, out_specs=out_specs, check_vma=False
    )
```

```python
import math

import jax
import jax.numpy as jnp
from jax import lax
from jax.experimental import pallas as pl
from jax.experimental.pallas import tpu as pltpu
from jax.sharding import PartitionSpec as P

DH = 128
KVH = 5
GQA = 8
TOKENS = 128
WIDTH = GQA * DH
PAIR = 2 * TOKENS
HALF = 64
SEEN = TOKENS + HALF
SIDE = 4
PLANE = SIDE * SIDE
FACTOR = 1.0 / math.sqrt(DH)
EXP_SCALE = FACTOR * math.log2(math.e)
LOW = -1e30
MESH = pl.DeviceIdType.MESH
F32 = jnp.float32
BF16 = jnp.bfloat16
LAST = (((1,), (1,)), ((), ()))


def dot_last(a, b):
    return lax.dot_general(a, b, LAST, preferred_element_type=F32)


def dot(a, b):
    return jnp.dot(a, b, preferred_element_type=F32)


def kernel(
    slots,
    len_ref, adv_ref, q_hbm, own_hbm, pre_hbm, do_hbm,
    qg, own_out, pre_out, scale_out,
    qs, dos, own, pre, own_k, own_v, pre_k, e_own, dp_own, stat, pt, dst, ogr, own_t,
    gat_own, gat_far, rs_out, rs_in, part, zs_out, zs_in, l_out, la_in, lb_in, lp_in, lz_in,
    in_sem, small_sem, z_send, z_recv, go_send, go_recv, gf_send, gf_recv, rs_send, rs_recv, zs_send, zs_recv, l_send, l_recv,
):
    group = lax.axis_index("group")
    resp = lax.axis_index("resp")
    vocab = lax.axis_index("vocab")
    half = resp % 2
    row = resp // 2

    ahead, behind = [None], [None]
    for d in range(1, PLANE):
        down, over = d // SIDE, d % SIDE
        ahead.append((group, ((row + down) % SIDE) * 2 + half, (vocab + over) % SIDE))
        behind.append((group, ((row + SIDE - down) % SIDE) * 2 + half, (vocab + SIDE - over) % SIDE))
    opposite = (group, row * 2 + 1 - half, vocab)
    near = [None] + [((group // 4) * 4 + (group + o) % 4, resp, vocab) for o in range(1, 4)]
    far = [None] + [((group + 4 * o) % 16, resp, vocab) for o in range(1, 4)]

    barrier = pltpu.get_barrier_semaphore()
    partners = [opposite] + ahead[1:] + near[1:] + far[1:]
    for partner in partners:
        pl.semaphore_signal(barrier, inc=1, device_id=partner, device_id_type=MESH)

    pre_copy = pltpu.make_async_copy(pre_hbm, pre, small_sem.at[0])
    own_copy = pltpu.make_async_copy(own_hbm, own, small_sem.at[1])
    pre_copy.start()
    own_copy.start()

    def in_copies(k):
        cols = pl.ds(pl.multiple_of(k * WIDTH, WIDTH), WIDTH)
        return (
            pltpu.make_async_copy(q_hbm.at[:, cols], qs.at[k], in_sem.at[0, k]),
            pltpu.make_async_copy(do_hbm.at[:, cols], dos.at[k], in_sem.at[1, k]),
        )

    for k in range(KVH):
        for copy in in_copies(k):
            copy.start()

    length = len_ref[0, 0]
    l_out[0] = jnp.full((8, DH), length.astype(F32))
    blank = jnp.zeros((8, DH), F32)
    pre_copy.wait()
    shard = pre[...].astype(F32)
    mine = []
    for k in range(KVH):
        cols = slice(k * DH, (k + 1) * DH)
        mine.append(jnp.concatenate([shard[:, 0, cols], shard[:, 1, cols]], axis=0))
    for t in range(3):
        low = mine[2 * t]
        high = mine[2 * t + 1] if 2 * t + 1 < KVH else blank
        gat_own[t, 0] = jnp.concatenate([low, high], axis=0).astype(BF16)

    def z_copy(t):
        return pltpu.make_async_remote_copy(
            src_ref=gat_own.at[t, 0], dst_ref=gat_far.at[t, 0], send_sem=z_send.at[t], recv_sem=z_recv.at[t],
            device_id=opposite, device_id_type=MESH,
        )

    def send(src, dst, sems, at, to):
        pltpu.make_async_remote_copy(
            src_ref=src, dst_ref=dst, send_sem=sems[0].at[at], recv_sem=sems[1].at[at],
            device_id=to, device_id_type=MESH,
        ).start()

    def landed(block, sems, at):
        return pltpu.make_async_remote_copy(
            src_ref=block, dst_ref=block, send_sem=sems[0].at[at], recv_sem=sems[1].at[at],
            device_id=opposite, device_id_type=MESH,
        )

    go_sems, gf_sems = (go_send, go_recv), (gf_send, gf_recv)
    l_sems, rs_sems = (l_send, l_recv), (rs_send, rs_recv)

    pl.semaphore_wait(barrier, len(partners))
    for t in range(3):
        z_copy(t).start()
    for d in range(1, PLANE):
        send(gat_own.at[:, 0], gat_own.at[:, d], go_sems, 0, ahead[d])
    for o in range(1, 4):
        send(l_out.at[0], la_in.at[o], l_sems, 0, near[o])

    own_copy.wait()
    own_rows = own[...]
    own_keys = own_rows[:, 0, :]
    own_values = own_rows[:, 1, :]
    for k in range(KVH):
        own_k[k] = own_keys[:, k * DH : (k + 1) * DH]
        own_v[k] = own_values[:, k * DH : (k + 1) * DH]

    lane = lax.broadcasted_iota(jnp.int32, (1, PAIR), 1) % TOKENS
    weight = jnp.where(lane < length, adv_ref[0, 0], 0.0)
    key_at = lax.broadcasted_iota(jnp.int32, (SEEN, PAIR), 0)
    query_at = lax.broadcasted_iota(jnp.int32, (SEEN, PAIR), 1) % TOKENS
    causal = (key_at <= query_at) | (key_at >= TOKENS)

    def pair_of(ref, k, c):
        return jnp.concatenate(
            [ref[k, :, (2 * c) * DH : (2 * c + 1) * DH], ref[k, :, (2 * c + 1) * DH : (2 * c + 2) * DH]], axis=0
        )

    def all_of(ref, k):
        return jnp.concatenate([ref[k, :, g * DH : (g + 1) * DH] for g in range(GQA)], axis=0)

    def rows_of(ref, k):
        tile = ref[k // 2].astype(F32)
        tile = jnp.where(k % 2 == 0, tile[:, 0:8, :], tile[:, 8:16, :])
        keys = [tile[s, 0:4] for s in range(PLANE)]
        values = [tile[s, 4:8] for s in range(PLANE)]
        return jnp.concatenate(keys, axis=0).astype(BF16), jnp.concatenate(values, axis=0).astype(BF16)

    def own_part(k):
        for copy in in_copies(k):
            copy.wait()
        plane_keys, plane_values = rows_of(gat_own, k)
        pre_k[k, 0:HALF] = plane_keys
        keys = jnp.concatenate([own_k[k], plane_keys], axis=0)
        values = jnp.concatenate([own_v[k], plane_values], axis=0)
        for c in range(GQA // 2):
            cols = slice(c * PAIR, (c + 1) * PAIR)
            score = jnp.where(causal, dot_last(keys, pair_of(qs, k, c)), LOW)
            peak = jnp.max(score, axis=0, keepdims=True)
            e = jnp.exp2((score - peak) * EXP_SCALE)
            dprob = dot_last(values, pair_of(dos, k, c))
            e_own[k, :, cols] = e
            dp_own[k, :, cols] = dprob
            stat[k, 0:1, cols] = peak
            stat[k, 1:2, cols] = jnp.sum(e, axis=0, keepdims=True)
            stat[k, 2:3, cols] = jnp.sum(e * dprob, axis=0, keepdims=True)

    def own_parts(start, stop):
        def step(k, carry):
            own_part(k)
            return carry

        lax.fori_loop(start, stop, step, 0)

    def spread_own_all():
        return landed(gat_own.at[:, pl.ds(1, PLANE - 1)], go_sems, 0)

    def spread(t):
        z_copy(t).wait_recv()
        for d in range(1, PLANE):
            send(gat_far.at[t, 0], gat_far.at[t, d], gf_sems, t, ahead[d])

    def spread_all(t):
        return landed(gat_far.at[t, pl.ds(1, PLANE - 1)], gf_sems, t)

    landed(la_in.at[pl.ds(1, 3)], l_sems, 0).wait_recv()
    l_out[1] = l_out[0] + la_in[1] + la_in[2] + la_in[3]
    for o in range(1, 4):
        send(l_out.at[1], lb_in.at[o], l_sems, 1, far[o])
    spread_own_all().wait_recv()
    own_part(0)
    for t in range(3):
        spread(t)
    own_parts(1, 2)
    landed(lb_in.at[pl.ds(1, 3)], l_sems, 1).wait_recv()
    l_out[2] = l_out[1] + lb_in[1] + lb_in[2] + lb_in[3]
    for d in range(1, PLANE):
        send(l_out.at[2], lp_in.at[d], l_sems, 2, ahead[d])
    own_parts(2, KVH)

    def scatter_all(k):
        return landed(rs_out.at[k, pl.ds(1, PLANE - 1)], rs_sems, k)

    def cross(k):
        return pltpu.make_async_remote_copy(
            src_ref=zs_out.at[k], dst_ref=zs_in.at[k], send_sem=zs_send.at[k], recv_sem=zs_recv.at[k],
            device_id=opposite, device_id_type=MESH,
        )

    def plane_sum(k):
        landed(rs_in.at[k, pl.ds(1, PLANE - 1)], rs_sems, k).wait_recv()
        total = part[k] + jnp.sum(rs_in[k, 1:PLANE].astype(F32), axis=0)
        part[k] = total
        zs_out[k] = total.astype(BF16)
        cross(k).start()

    length_cross = pltpu.make_async_remote_copy(
        src_ref=l_out.at[3], dst_ref=lz_in, send_sem=l_send.at[3], recv_sem=l_recv.at[3],
        device_id=opposite, device_id_type=MESH,
    )

    def prefix_part(k, carry):
        @pl.when(k == 0)
        def _():
            spread_all(0).wait_recv()

        @pl.when(k == 2)
        def _():
            spread_all(1).wait_recv()

        @pl.when(k == 4)
        def _():
            spread_all(2).wait_recv()

        keys, values = rows_of(gat_far, k)
        pre_k[k, HALF:TOKENS] = keys
        for c in range(GQA // 2):
            cols = slice(c * PAIR, (c + 1) * PAIR)
            score = dot_last(keys, pair_of(qs, k, c))
            own_peak = stat[k, 0:1, cols]
            peak = jnp.maximum(own_peak, jnp.max(score, axis=0, keepdims=True))
            e = jnp.exp2((score - peak) * EXP_SCALE)
            dprob = dot_last(values, pair_of(dos, k, c))
            shrink = jnp.exp2((own_peak - peak) * EXP_SCALE)
            inverse = 1.0 / (jnp.sum(e, axis=0, keepdims=True) + shrink * stat[k, 1:2, cols])
            delta = (jnp.sum(e * dprob, axis=0, keepdims=True) + shrink * stat[k, 2:3, cols]) * inverse
            scaled = inverse * weight
            own_scaled = shrink * scaled
            near_prob = e_own[k, TOKENS:SEEN, cols] * own_scaled
            far_prob = e * scaled
            pt[0:HALF, cols] = near_prob.astype(BF16)
            pt[HALF:TOKENS, cols] = far_prob.astype(BF16)
            dst[k, 0:HALF, cols] = (near_prob * (dp_own[k, TOKENS:SEEN, cols] - delta)).astype(BF16)
            dst[k, HALF:TOKENS, cols] = (far_prob * (dprob - delta)).astype(BF16)
            stat[k, 3:4, cols] = own_scaled
            stat[k, 4:5, cols] = delta
        grad_k = dot(dst[k, 0:TOKENS, :], all_of(qs, k)) * FACTOR
        grad_v = dot(pt[...], all_of(dos, k))
        for d in range(PLANE):
            near_rows, far_rows = slice(4 * d, 4 * d + 4), slice(HALF + 4 * d, HALF + 4 * d + 4)
            tile = jnp.concatenate(
                [grad_k[near_rows], grad_k[far_rows], grad_v[near_rows], grad_v[far_rows]], axis=0
            )
            if d == 0:
                part[k] = tile
            else:
                rs_out[k, d] = tile.astype(BF16)
        for d in range(1, PLANE):
            send(rs_out.at[k, d], rs_in.at[k, d], rs_sems, k, behind[d])

        @pl.when(k >= 2)
        def _():
            plane_sum(k - 2)

        @pl.when(k == 1)
        def _():
            landed(lp_in.at[pl.ds(1, PLANE - 1)], l_sems, 2).wait_recv()
            l_out[3] = l_out[2] + jnp.sum(lp_in[1:PLANE], axis=0)
            length_cross.start()

        return carry

    lax.fori_loop(0, KVH, prefix_part, 0)

    def own_grads(k):
        for c in range(GQA // 2):
            cols = slice(c * PAIR, (c + 1) * PAIR)
            prob = e_own[k, 0:TOKENS, cols] * stat[k, 3:4, cols]
            pt[:, cols] = prob.astype(BF16)
            dst[k, TOKENS:PAIR, cols] = (prob * (dp_own[k, 0:TOKENS, cols] - stat[k, 4:5, cols])).astype(BF16)
        ogr[k, 0] = dot(dst[k, TOKENS:PAIR, :], all_of(qs, k)) * FACTOR
        ogr[k, 1] = dot(pt[...], all_of(dos, k))

    def own_grads_step(k, carry):
        own_grads(k)
        return carry

    own_grads(0)
    plane_sum(3)
    own_grads(1)
    plane_sum(4)
    lax.fori_loop(2, KVH, own_grads_step, 0)
    length_cross.wait_recv()
    scale = slots / (l_out[3] + lz_in[...])
    scale_out[...] = scale[0:1, 0:1]
    one = scale[0:1, :]
    one_k = one * FACTOR

    def query_grads(k, carry):
        head = pl.ds(pl.multiple_of(k * DH, DH), DH)
        own_t[0, :, head] = (ogr[k, 0] * one).astype(BF16)
        own_t[1, :, head] = (ogr[k, 1] * one).astype(BF16)
        keys = jnp.concatenate([pre_k[k].astype(F32).T, own_k[k].astype(F32).T], axis=1).astype(BF16)
        for c in range(GQA // 2):
            turned = dot(keys, dst[k, :, c * PAIR : (c + 1) * PAIR])
            for g in range(2):
                at = pl.ds(pl.multiple_of(k * WIDTH + (2 * c + g) * DH, DH), DH)
                qg[:, at] = (turned[:, g * DH : (g + 1) * DH].T * one_k).astype(BF16)
        return carry

    lax.fori_loop(0, KVH, query_grads, 0)
    own_out[:, 0, :] = own_t[0]
    own_out[:, 1, :] = own_t[1]

    for k in range(KVH):
        cols = slice(k * DH, (k + 1) * DH)
        cross(k).wait_recv()
        there = zs_in[k].astype(F32)
        pre_out[:, 0, cols] = (part[k, 0:4] + there[4:8]) * one
        pre_out[:, 1, cols] = (part[k, 8:12] + there[12:16]) * one

    for k in range(KVH):
        scatter_all(k).wait_send()
        cross(k).wait_send()
    spread_own_all().wait_send()
    for t in range(3):
        spread_all(t).wait_send()
        z_copy(t).wait_send()
    for at in range(2):
        landed(la_in.at[pl.ds(1, 3)], l_sems, at).wait_send()
    landed(lp_in.at[pl.ds(1, PLANE - 1)], l_sems, 2).wait_send()
    length_cross.wait_send()


def write_out(qg, own, pre, qg_out, own_out, pre_out, sems):
    copies = [pltpu.make_async_copy(pre, pre_out, sems.at[0])]
    for at in range(8):
        rows = pl.ds(16 * at, 16)
        copies.append(pltpu.make_async_copy(qg.at[rows], qg_out.at[rows], sems.at[1 + at]))
    for at in range(2):
        rows = pl.ds(64 * at, 64)
        copies.append(pltpu.make_async_copy(own.at[rows], own_out.at[rows], sems.at[9 + at]))
    for copy in copies:
        copy.start()
    for copy in copies:
        copy.wait()


def on_device(queries, own_kv, prefix_kv, out_grad, lengths, advantages):
    slots = float(
        queries.shape[2] * lax.axis_size("group") * lax.axis_size("resp") * lax.axis_size("vocab")
    )
    width = KVH * WIDTH
    vmem = pltpu.VMEM
    dma = pltpu.SemaphoreType.DMA
    in_hbm = pl.BlockSpec(memory_space=pltpu.HBM)
    in_smem = pl.BlockSpec(memory_space=pltpu.SMEM)
    in_vmem = pl.BlockSpec(memory_space=pltpu.VMEM)

    def body(*refs):
        kernel(slots, *refs)

    def held(x):
        return pltpu.with_memory_space_constraint(x, pltpu.HBM)

    query_shape, own_shape, prefix_shape = (TOKENS, width), (TOKENS, 2, KVH * DH), (4, 2, KVH * DH)
    query_grad, own_grad, prefix_grad, token_scale = pl.pallas_call(
        body,
        out_shape=(
            vmem(query_shape, BF16),
            vmem(own_shape, BF16),
            vmem(prefix_shape, F32),
            jax.ShapeDtypeStruct((1, 1), F32),
        ),
        in_specs=[in_smem, in_smem, in_hbm, in_hbm, in_hbm, in_hbm],
        out_specs=(in_vmem, in_vmem, in_vmem, in_vmem),
        scratch_shapes=[
            vmem((KVH, TOKENS, WIDTH), BF16),
            vmem((KVH, TOKENS, WIDTH), BF16),
            vmem((TOKENS, 2, KVH * DH), BF16),
            vmem((4, 2, KVH * DH), BF16),
            vmem((KVH, TOKENS, DH), BF16),
            vmem((KVH, TOKENS, DH), BF16),
            vmem((KVH, TOKENS, DH), BF16),
            vmem((KVH, SEEN, WIDTH), F32),
            vmem((KVH, SEEN, WIDTH), F32),
            vmem((KVH, 8, WIDTH), F32),
            vmem((TOKENS, WIDTH), BF16),
            vmem((KVH, PAIR, WIDTH), BF16),
            vmem((KVH, 2, TOKENS, DH), F32),
            vmem((2, TOKENS, KVH * DH), BF16),
            vmem((3, PLANE, 16, DH), BF16),
            vmem((3, PLANE, 16, DH), BF16),
            vmem((KVH, PLANE, 16, DH), BF16),
            vmem((KVH, PLANE, 16, DH), BF16),
            vmem((KVH, 16, DH), F32),
            vmem((KVH, 16, DH), BF16),
            vmem((KVH, 16, DH), BF16),
            vmem((4, 8, DH), F32),
            vmem((4, 8, DH), F32),
            vmem((4, 8, DH), F32),
            vmem((PLANE, 8, DH), F32),
            vmem((8, DH), F32),
            dma((2, KVH)),
            dma((2,)),
            dma((3,)),
            dma((3,)),
            dma((1,)),
            dma((1,)),
            dma((3,)),
            dma((3,)),
            dma((KVH,)),
            dma((KVH,)),
            dma((KVH,)),
            dma((KVH,)),
            dma((4,)),
            dma((4,)),
        ],
        compiler_params=pltpu.CompilerParams(
            collective_id=0, has_side_effects=True, vmem_limit_bytes=48 * 1024 * 1024
        ),
        cost_estimate=pl.CostEstimate(
            flops=5 * KVH * 2 * WIDTH * PAIR * DH,
            bytes_accessed=5 * 1024 * 1024,
            transcendentals=KVH * WIDTH * PAIR,
        ),
    )(lengths, advantages, held(queries[0, 0]), held(own_kv[0, 0]), held(prefix_kv[0]), held(out_grad[0, 0]))
    query_grad, own_grad, prefix_grad = pl.pallas_call(
        write_out,
        out_shape=(
            jax.ShapeDtypeStruct(query_shape, BF16),
            jax.ShapeDtypeStruct(own_shape, BF16),
            jax.ShapeDtypeStruct(prefix_shape, F32),
        ),
        in_specs=[in_vmem] * 3,
        out_specs=(in_hbm,) * 3,
        scratch_shapes=[dma((11,))],
        compiler_params=pltpu.CompilerParams(vmem_limit_bytes=8 * 1024 * 1024),
    )(query_grad, own_grad, prefix_grad)
    return query_grad[None, None], own_grad[None, None], prefix_grad[None], token_scale[0, 0]


def solution(mesh):
    in_specs = (
        P("group", ("resp", "vocab"), None, None),
        P("group", ("resp", "vocab"), None, None, None),
        P("group", ("resp", "vocab"), None, None),
        P("group", ("resp", "vocab"), None, None),
        P("group", ("resp", "vocab")),
        P("group", ("resp", "vocab")),
    )
    out_specs = (
        P("group", ("resp", "vocab"), None, None),
        P("group", ("resp", "vocab"), None, None, None),
        P("group", ("resp", "vocab"), None, None),
        P(),
    )
    return jax.shard_map(
        on_device, mesh=mesh, in_specs=in_specs, out_specs=out_specs, check_vma=False
    )
```

```python
import math

import jax
import jax.numpy as jnp
from jax import lax
from jax.experimental import pallas as pl
from jax.experimental.pallas import tpu as pltpu
from jax.sharding import PartitionSpec as P

DH = 128
KVH = 5
GQA = 8
TOKENS = 128
WIDTH = GQA * DH
PAIR = 2 * TOKENS
HALF = 64
SEEN = TOKENS + HALF
SIDE = 4
PLANE = SIDE * SIDE
FACTOR = 1.0 / math.sqrt(DH)
EXP_SCALE = FACTOR * math.log2(math.e)
LOW = -1e30
MESH = pl.DeviceIdType.MESH
F32 = jnp.float32
BF16 = jnp.bfloat16
LAST = (((1,), (1,)), ((), ()))


def dot_last(a, b):
    return lax.dot_general(a, b, LAST, preferred_element_type=F32)


def dot(a, b):
    return jnp.dot(a, b, preferred_element_type=F32)


def kernel(
    slots,
    len_ref, adv_ref, q_hbm, own_hbm, pre_hbm, do_hbm,
    qg, own_out, pre_out, scale_out,
    qs, dos, own, pre, own_k, own_v, pre_k, e_own, dp_own, stat, pt, dst, ogr, own_t,
    gat_own, gat_far, rs_out, rs_in, part, zs_out, zs_in, l_out, la_in, lb_in, lp_in,
    in_sem, small_sem, z_send, z_recv, go_send, go_recv, gf_send, gf_recv, rs_send, rs_recv, zs_send, zs_recv, l_send, l_recv,
):
    group = lax.axis_index("group")
    resp = lax.axis_index("resp")
    vocab = lax.axis_index("vocab")
    half = resp % 2
    row = resp // 2

    ahead, behind = [None], [None]
    for d in range(1, PLANE):
        down, over = d // SIDE, d % SIDE
        ahead.append((group, ((row + down) % SIDE) * 2 + half, (vocab + over) % SIDE))
        behind.append((group, ((row + SIDE - down) % SIDE) * 2 + half, (vocab + SIDE - over) % SIDE))
    opposite = (group, row * 2 + 1 - half, vocab)
    near = [None] + [((group // 4) * 4 + (group + o) % 4, resp, vocab) for o in range(1, 4)]
    far = [None] + [((group + 4 * o) % 16, resp, vocab) for o in range(1, 4)]
    far += [((group + 4 * o) % 16, row * 2 + 1 - half, vocab) for o in range(4)]

    barrier = pltpu.get_barrier_semaphore()
    partners = [opposite] + ahead[1:] + near[1:] + far[1:4] + far[5:]
    for partner in partners:
        pl.semaphore_signal(barrier, inc=1, device_id=partner, device_id_type=MESH)

    pre_copy = pltpu.make_async_copy(pre_hbm, pre, small_sem.at[0])
    own_copy = pltpu.make_async_copy(own_hbm, own, small_sem.at[1])
    pre_copy.start()
    own_copy.start()

    def in_copies(k):
        cols = pl.ds(pl.multiple_of(k * WIDTH, WIDTH), WIDTH)
        return (
            pltpu.make_async_copy(q_hbm.at[:, cols], qs.at[k], in_sem.at[0, k]),
            pltpu.make_async_copy(do_hbm.at[:, cols], dos.at[k], in_sem.at[1, k]),
        )

    for k in range(KVH):
        for copy in in_copies(k):
            copy.start()

    length = len_ref[0, 0]
    l_out[0] = jnp.full((8, DH), length.astype(F32))
    blank = jnp.zeros((8, DH), F32)
    pre_copy.wait()
    shard = pre[...].astype(F32)
    mine = []
    for k in range(KVH):
        cols = slice(k * DH, (k + 1) * DH)
        mine.append(jnp.concatenate([shard[:, 0, cols], shard[:, 1, cols]], axis=0))
    for t in range(3):
        low = mine[2 * t]
        high = mine[2 * t + 1] if 2 * t + 1 < KVH else blank
        gat_own[t, 0] = jnp.concatenate([low, high], axis=0).astype(BF16)

    def z_copy(t):
        return pltpu.make_async_remote_copy(
            src_ref=gat_own.at[t, 0], dst_ref=gat_far.at[t, 0], send_sem=z_send.at[t], recv_sem=z_recv.at[t],
            device_id=opposite, device_id_type=MESH,
        )

    def send(src, dst, sems, at, to):
        pltpu.make_async_remote_copy(
            src_ref=src, dst_ref=dst, send_sem=sems[0].at[at], recv_sem=sems[1].at[at],
            device_id=to, device_id_type=MESH,
        ).start()

    def landed(block, sems, at):
        return pltpu.make_async_remote_copy(
            src_ref=block, dst_ref=block, send_sem=sems[0].at[at], recv_sem=sems[1].at[at],
            device_id=opposite, device_id_type=MESH,
        )

    go_sems, gf_sems = (go_send, go_recv), (gf_send, gf_recv)
    l_sems, rs_sems = (l_send, l_recv), (rs_send, rs_recv)

    pl.semaphore_wait(barrier, len(partners))
    for t in range(3):
        z_copy(t).start()
    for d in range(1, PLANE):
        send(gat_own.at[:, 0], gat_own.at[:, d], go_sems, 0, ahead[d])
    for o in range(1, 4):
        send(l_out.at[0], la_in.at[o], l_sems, 0, near[o])

    own_copy.wait()
    own_rows = own[...]
    own_keys = own_rows[:, 0, :]
    own_values = own_rows[:, 1, :]
    for k in range(KVH):
        own_k[k] = own_keys[:, k * DH : (k + 1) * DH]
        own_v[k] = own_values[:, k * DH : (k + 1) * DH]

    lane = lax.broadcasted_iota(jnp.int32, (1, PAIR), 1) % TOKENS
    weight = jnp.where(lane < length, adv_ref[0, 0], 0.0)
    key_at = lax.broadcasted_iota(jnp.int32, (SEEN, PAIR), 0)
    query_at = lax.broadcasted_iota(jnp.int32, (SEEN, PAIR), 1) % TOKENS
    causal = (key_at <= query_at) | (key_at >= TOKENS)

    def pair_of(ref, k, c):
        return jnp.concatenate(
            [ref[k, :, (2 * c) * DH : (2 * c + 1) * DH], ref[k, :, (2 * c + 1) * DH : (2 * c + 2) * DH]], axis=0
        )

    def all_of(ref, k):
        return jnp.concatenate([ref[k, :, g * DH : (g + 1) * DH] for g in range(GQA)], axis=0)

    def rows_of(ref, k):
        tile = ref[k // 2].astype(F32)
        tile = jnp.where(k % 2 == 0, tile[:, 0:8, :], tile[:, 8:16, :])
        keys = [tile[s, 0:4] for s in range(PLANE)]
        values = [tile[s, 4:8] for s in range(PLANE)]
        return jnp.concatenate(keys, axis=0).astype(BF16), jnp.concatenate(values, axis=0).astype(BF16)

    def own_part(k):
        for copy in in_copies(k):
            copy.wait()
        plane_keys, plane_values = rows_of(gat_own, k)
        pre_k[k, 0:HALF] = plane_keys
        keys = jnp.concatenate([own_k[k], plane_keys], axis=0)
        values = jnp.concatenate([own_v[k], plane_values], axis=0)
        for c in range(GQA // 2):
            cols = slice(c * PAIR, (c + 1) * PAIR)
            score = jnp.where(causal, dot_last(keys, pair_of(qs, k, c)), LOW)
            peak = jnp.max(score, axis=0, keepdims=True)
            e = jnp.exp2((score - peak) * EXP_SCALE)
            dprob = dot_last(values, pair_of(dos, k, c))
            e_own[k, :, cols] = e
            dp_own[k, :, cols] = dprob
            stat[k, 0:1, cols] = peak
            stat[k, 1:2, cols] = jnp.sum(e, axis=0, keepdims=True)
            stat[k, 2:3, cols] = jnp.sum(e * dprob, axis=0, keepdims=True)

    def own_parts(start, stop):
        def step(k, carry):
            own_part(k)
            return carry

        lax.fori_loop(start, stop, step, 0)

    def spread_own_all():
        return landed(gat_own.at[:, pl.ds(1, PLANE - 1)], go_sems, 0)

    def spread(t):
        z_copy(t).wait_recv()
        for d in range(1, PLANE):
            send(gat_far.at[t, 0], gat_far.at[t, d], gf_sems, t, ahead[d])

    def spread_all(t):
        return landed(gat_far.at[t, pl.ds(1, PLANE - 1)], gf_sems, t)

    landed(la_in.at[pl.ds(1, 3)], l_sems, 0).wait_recv()
    l_out[1] = l_out[0] + la_in[1] + la_in[2] + la_in[3]
    for o in range(1, 8):
        send(l_out.at[1], lb_in.at[o], l_sems, 1, far[o])
    spread_own_all().wait_recv()
    own_part(0)
    for t in range(3):
        spread(t)
    own_parts(1, 3)
    landed(lb_in.at[pl.ds(1, 7)], l_sems, 1).wait_recv()
    l_out[2] = l_out[1] + jnp.sum(lb_in[1:8], axis=0)
    for d in range(1, PLANE):
        send(l_out.at[2], lp_in.at[d], l_sems, 2, ahead[d])
    own_parts(3, KVH)

    def scatter_all(k):
        return landed(rs_out.at[k, pl.ds(1, PLANE - 1)], rs_sems, k)

    def cross(k):
        return pltpu.make_async_remote_copy(
            src_ref=zs_out.at[k], dst_ref=zs_in.at[k], send_sem=zs_send.at[k], recv_sem=zs_recv.at[k],
            device_id=opposite, device_id_type=MESH,
        )

    def plane_sum(k):
        landed(rs_in.at[k, pl.ds(1, PLANE - 1)], rs_sems, k).wait_recv()
        total = part[k] + jnp.sum(rs_in[k, 1:PLANE].astype(F32), axis=0)
        part[k] = total
        zs_out[k] = total.astype(BF16)
        cross(k).start()

    def prefix_part(k, carry):
        @pl.when(k == 0)
        def _():
            spread_all(0).wait_recv()

        @pl.when(k == 2)
        def _():
            spread_all(1).wait_recv()

        @pl.when(k == 4)
        def _():
            spread_all(2).wait_recv()

        keys, values = rows_of(gat_far, k)
        pre_k[k, HALF:TOKENS] = keys
        for c in range(GQA // 2):
            cols = slice(c * PAIR, (c + 1) * PAIR)
            score = dot_last(keys, pair_of(qs, k, c))
            own_peak = stat[k, 0:1, cols]
            peak = jnp.maximum(own_peak, jnp.max(score, axis=0, keepdims=True))
            e = jnp.exp2((score - peak) * EXP_SCALE)
            dprob = dot_last(values, pair_of(dos, k, c))
            shrink = jnp.exp2((own_peak - peak) * EXP_SCALE)
            inverse = 1.0 / (jnp.sum(e, axis=0, keepdims=True) + shrink * stat[k, 1:2, cols])
            delta = (jnp.sum(e * dprob, axis=0, keepdims=True) + shrink * stat[k, 2:3, cols]) * inverse
            scaled = inverse * weight
            own_scaled = shrink * scaled
            near_prob = e_own[k, TOKENS:SEEN, cols] * own_scaled
            far_prob = e * scaled
            pt[0:HALF, cols] = near_prob.astype(BF16)
            pt[HALF:TOKENS, cols] = far_prob.astype(BF16)
            dst[k, 0:HALF, cols] = (near_prob * (dp_own[k, TOKENS:SEEN, cols] - delta)).astype(BF16)
            dst[k, HALF:TOKENS, cols] = (far_prob * (dprob - delta)).astype(BF16)
            stat[k, 3:4, cols] = own_scaled
            stat[k, 4:5, cols] = delta
        grad_k = dot(dst[k, 0:TOKENS, :], all_of(qs, k)) * FACTOR
        grad_v = dot(pt[...], all_of(dos, k))
        for d in range(PLANE):
            near_rows, far_rows = slice(4 * d, 4 * d + 4), slice(HALF + 4 * d, HALF + 4 * d + 4)
            tile = jnp.concatenate(
                [grad_k[near_rows], grad_k[far_rows], grad_v[near_rows], grad_v[far_rows]], axis=0
            )
            if d == 0:
                part[k] = tile
            else:
                rs_out[k, d] = tile.astype(BF16)
        for d in range(1, PLANE):
            send(rs_out.at[k, d], rs_in.at[k, d], rs_sems, k, behind[d])

        return carry

    lax.fori_loop(0, KVH, prefix_part, 0)

    def own_grads(k):
        for c in range(GQA // 2):
            cols = slice(c * PAIR, (c + 1) * PAIR)
            prob = e_own[k, 0:TOKENS, cols] * stat[k, 3:4, cols]
            pt[:, cols] = prob.astype(BF16)
            dst[k, TOKENS:PAIR, cols] = (prob * (dp_own[k, 0:TOKENS, cols] - stat[k, 4:5, cols])).astype(BF16)
        ogr[k, 0] = dot(dst[k, TOKENS:PAIR, :], all_of(qs, k)) * FACTOR
        ogr[k, 1] = dot(pt[...], all_of(dos, k))

    def own_grads_step(k, carry):
        own_grads(k)
        return carry

    def plane_sum_step(k, carry):
        plane_sum(k)
        return carry

    lax.fori_loop(0, 3, own_grads_step, 0)
    lax.fori_loop(0, 3, plane_sum_step, 0)
    lax.fori_loop(3, 4, own_grads_step, 0)
    lax.fori_loop(3, KVH, plane_sum_step, 0)
    lax.fori_loop(4, KVH, own_grads_step, 0)
    landed(lp_in.at[pl.ds(1, PLANE - 1)], l_sems, 2).wait_recv()
    scale = slots / (l_out[2] + jnp.sum(lp_in[1:PLANE], axis=0))
    scale_out[...] = scale
    one = scale[0:1, :]
    one_k = one * FACTOR

    def query_grads(k, carry):
        head = pl.ds(pl.multiple_of(k * DH, DH), DH)
        own_t[0, :, head] = (ogr[k, 0] * one).astype(BF16)
        own_t[1, :, head] = (ogr[k, 1] * one).astype(BF16)
        keys = jnp.concatenate([pre_k[k].astype(F32).T, own_k[k].astype(F32).T], axis=1).astype(BF16)
        for c in range(GQA // 2):
            turned = dot(keys, dst[k, :, c * PAIR : (c + 1) * PAIR])
            for g in range(2):
                at = pl.ds(pl.multiple_of(k * WIDTH + (2 * c + g) * DH, DH), DH)
                qg[:, at] = (turned[:, g * DH : (g + 1) * DH].T * one_k).astype(BF16)
        return carry

    lax.fori_loop(0, KVH, query_grads, 0)
    own_out[:, 0, :] = own_t[0]
    own_out[:, 1, :] = own_t[1]

    for k in range(KVH):
        cols = slice(k * DH, (k + 1) * DH)
        cross(k).wait_recv()
        there = zs_in[k].astype(F32)
        pre_out[:, 0, cols] = (part[k, 0:4] + there[4:8]) * one
        pre_out[:, 1, cols] = (part[k, 8:12] + there[12:16]) * one

    for k in range(KVH):
        scatter_all(k).wait_send()
        cross(k).wait_send()
    spread_own_all().wait_send()
    for t in range(3):
        spread_all(t).wait_send()
        z_copy(t).wait_send()
    landed(la_in.at[pl.ds(1, 3)], l_sems, 0).wait_send()
    landed(lb_in.at[pl.ds(1, 7)], l_sems, 1).wait_send()
    landed(lp_in.at[pl.ds(1, PLANE - 1)], l_sems, 2).wait_send()


def write_out(qg, own, pre, scale, qg_out, own_out, pre_out, scale_out, one, sems):
    one[...] = scale[0:1, 0:1]
    copies = [
        pltpu.make_async_copy(pre, pre_out, sems.at[0]),
        pltpu.make_async_copy(one, scale_out, sems.at[11]),
    ]
    for at in range(8):
        rows = pl.ds(16 * at, 16)
        copies.append(pltpu.make_async_copy(qg.at[rows], qg_out.at[rows], sems.at[1 + at]))
    for at in range(2):
        rows = pl.ds(64 * at, 64)
        copies.append(pltpu.make_async_copy(own.at[rows], own_out.at[rows], sems.at[9 + at]))
    for copy in copies:
        copy.start()
    for copy in copies:
        copy.wait()


def on_device(queries, own_kv, prefix_kv, out_grad, lengths, advantages):
    slots = float(
        queries.shape[2] * lax.axis_size("group") * lax.axis_size("resp") * lax.axis_size("vocab")
    )
    width = KVH * WIDTH
    vmem = pltpu.VMEM
    dma = pltpu.SemaphoreType.DMA
    in_hbm = pl.BlockSpec(memory_space=pltpu.HBM)
    in_smem = pl.BlockSpec(memory_space=pltpu.SMEM)
    in_vmem = pl.BlockSpec(memory_space=pltpu.VMEM)

    def body(*refs):
        kernel(slots, *refs)

    def held(x):
        return pltpu.with_memory_space_constraint(x, pltpu.HBM)

    query_shape, own_shape, prefix_shape = (TOKENS, width), (TOKENS, 2, KVH * DH), (4, 2, KVH * DH)
    query_grad, own_grad, prefix_grad, token_scale = pl.pallas_call(
        body,
        out_shape=(
            vmem(query_shape, BF16),
            vmem(own_shape, BF16),
            vmem(prefix_shape, F32),
            vmem((8, DH), F32),
        ),
        in_specs=[in_smem, in_smem, in_hbm, in_hbm, in_hbm, in_hbm],
        out_specs=(in_vmem, in_vmem, in_vmem, in_vmem),
        scratch_shapes=[
            vmem((KVH, TOKENS, WIDTH), BF16),
            vmem((KVH, TOKENS, WIDTH), BF16),
            vmem((TOKENS, 2, KVH * DH), BF16),
            vmem((4, 2, KVH * DH), BF16),
            vmem((KVH, TOKENS, DH), BF16),
            vmem((KVH, TOKENS, DH), BF16),
            vmem((KVH, TOKENS, DH), BF16),
            vmem((KVH, SEEN, WIDTH), F32),
            vmem((KVH, SEEN, WIDTH), F32),
            vmem((KVH, 8, WIDTH), F32),
            vmem((TOKENS, WIDTH), BF16),
            vmem((KVH, PAIR, WIDTH), BF16),
            vmem((KVH, 2, TOKENS, DH), F32),
            vmem((2, TOKENS, KVH * DH), BF16),
            vmem((3, PLANE, 16, DH), BF16),
            vmem((3, PLANE, 16, DH), BF16),
            vmem((KVH, PLANE, 16, DH), BF16),
            vmem((KVH, PLANE, 16, DH), BF16),
            vmem((KVH, 16, DH), F32),
            vmem((KVH, 16, DH), BF16),
            vmem((KVH, 16, DH), BF16),
            vmem((3, 8, DH), F32),
            vmem((4, 8, DH), F32),
            vmem((8, 8, DH), F32),
            vmem((PLANE, 8, DH), F32),
            dma((2, KVH)),
            dma((2,)),
            dma((3,)),
            dma((3,)),
            dma((1,)),
            dma((1,)),
            dma((3,)),
            dma((3,)),
            dma((KVH,)),
            dma((KVH,)),
            dma((KVH,)),
            dma((KVH,)),
            dma((3,)),
            dma((3,)),
        ],
        compiler_params=pltpu.CompilerParams(
            collective_id=0, has_side_effects=True, vmem_limit_bytes=48 * 1024 * 1024
        ),
        cost_estimate=pl.CostEstimate(
            flops=5 * KVH * 2 * WIDTH * PAIR * DH,
            bytes_accessed=5 * 1024 * 1024,
            transcendentals=KVH * WIDTH * PAIR,
        ),
    )(lengths, advantages, held(queries[0, 0]), held(own_kv[0, 0]), held(prefix_kv[0]), held(out_grad[0, 0]))
    query_grad, own_grad, prefix_grad, token_scale = pl.pallas_call(
        write_out,
        out_shape=(
            jax.ShapeDtypeStruct(query_shape, BF16),
            jax.ShapeDtypeStruct(own_shape, BF16),
            jax.ShapeDtypeStruct(prefix_shape, F32),
            jax.ShapeDtypeStruct((1, 1), F32),
        ),
        in_specs=[in_vmem] * 4,
        out_specs=(in_hbm,) * 4,
        scratch_shapes=[vmem((1, 1), F32), dma((12,))],
        compiler_params=pltpu.CompilerParams(vmem_limit_bytes=8 * 1024 * 1024),
    )(query_grad, own_grad, prefix_grad, token_scale)
    return query_grad[None, None], own_grad[None, None], prefix_grad[None], token_scale[0, 0]


def solution(mesh):
    in_specs = (
        P("group", ("resp", "vocab"), None, None),
        P("group", ("resp", "vocab"), None, None, None),
        P("group", ("resp", "vocab"), None, None),
        P("group", ("resp", "vocab"), None, None),
        P("group", ("resp", "vocab")),
        P("group", ("resp", "vocab")),
    )
    out_specs = (
        P("group", ("resp", "vocab"), None, None),
        P("group", ("resp", "vocab"), None, None, None),
        P("group", ("resp", "vocab"), None, None),
        P(),
    )
    return jax.shard_map(
        on_device, mesh=mesh, in_specs=in_specs, out_specs=out_specs, check_vma=False
    )
```

```python
import math

import jax
import jax.numpy as jnp
from jax import lax
from jax.experimental import pallas as pl
from jax.experimental.pallas import tpu as pltpu
from jax.sharding import PartitionSpec as P

DH = 128
KVH = 5
GQA = 8
TOKENS = 128
WIDTH = GQA * DH
PAIR = 2 * TOKENS
HALF = 64
SEEN = TOKENS + HALF
SIDE = 4
PLANE = SIDE * SIDE
FACTOR = 1.0 / math.sqrt(DH)
EXP_SCALE = FACTOR * math.log2(math.e)
LOW = -1e30
MESH = pl.DeviceIdType.MESH
F32 = jnp.float32
BF16 = jnp.bfloat16
LAST = (((1,), (1,)), ((), ()))


def dot_last(a, b):
    return lax.dot_general(a, b, LAST, preferred_element_type=F32)


def dot(a, b):
    return jnp.dot(a, b, preferred_element_type=F32)


def kernel(
    slots,
    len_ref, adv_ref, q_hbm, own_hbm, pre_hbm, do_hbm,
    qg, own_out, pre_out, scale_out,
    qs, dos, own, pre, own_k, own_v, pre_k, e_own, dp_own, stat, pt, dst, ogr, own_t,
    gat_own, gat_far, rs_out, rs_in, part, zs_out, zs_in, l_out, la_in, lb_in, lp_in,
    in_sem, small_sem, z_send, z_recv, go_send, go_recv, gf_send, gf_recv, rs_send, rs_recv, zs_send, zs_recv, l_send, l_recv,
):
    group = lax.axis_index("group")
    resp = lax.axis_index("resp")
    vocab = lax.axis_index("vocab")
    half = resp % 2
    row = resp // 2

    ahead, behind = [None], [None]
    for d in range(1, PLANE):
        down, over = d // SIDE, d % SIDE
        ahead.append((group, ((row + down) % SIDE) * 2 + half, (vocab + over) % SIDE))
        behind.append((group, ((row + SIDE - down) % SIDE) * 2 + half, (vocab + SIDE - over) % SIDE))
    opposite = (group, row * 2 + 1 - half, vocab)
    near = [None] + [((group // 4) * 4 + (group + o) % 4, resp, vocab) for o in range(1, 4)]
    far = [None] + [((group + 4 * o) % 16, resp, vocab) for o in range(1, 4)]
    far += [((group + 4 * o) % 16, row * 2 + 1 - half, vocab) for o in range(4)]

    barrier = pltpu.get_barrier_semaphore()
    partners = [opposite] + ahead[1:] + near[1:] + far[1:4] + far[5:]
    for partner in partners:
        pl.semaphore_signal(barrier, inc=1, device_id=partner, device_id_type=MESH)

    pre_copy = pltpu.make_async_copy(pre_hbm, pre, small_sem.at[0])
    own_copy = pltpu.make_async_copy(own_hbm, own, small_sem.at[1])
    pre_copy.start()
    own_copy.start()

    def in_copies(k):
        cols = pl.ds(pl.multiple_of(k * WIDTH, WIDTH), WIDTH)
        return (
            pltpu.make_async_copy(q_hbm.at[:, cols], qs.at[k], in_sem.at[0, k]),
            pltpu.make_async_copy(do_hbm.at[:, cols], dos.at[k], in_sem.at[1, k]),
        )

    for k in range(KVH):
        for copy in in_copies(k):
            copy.start()

    length = len_ref[0, 0]
    l_out[0] = jnp.full((8, DH), length.astype(F32))
    blank = jnp.zeros((8, DH), F32)
    pre_copy.wait()
    shard = pre[...].astype(F32)
    mine = []
    for k in range(KVH):
        cols = slice(k * DH, (k + 1) * DH)
        mine.append(jnp.concatenate([shard[:, 0, cols], shard[:, 1, cols]], axis=0))
    for t in range(3):
        low = mine[2 * t]
        high = mine[2 * t + 1] if 2 * t + 1 < KVH else blank
        gat_own[t, 0] = jnp.concatenate([low, high], axis=0).astype(BF16)

    def z_copy(t):
        return pltpu.make_async_remote_copy(
            src_ref=gat_own.at[t, 0], dst_ref=gat_far.at[t, 0], send_sem=z_send.at[t], recv_sem=z_recv.at[t],
            device_id=opposite, device_id_type=MESH,
        )

    def send(src, dst, sems, at, to):
        pltpu.make_async_remote_copy(
            src_ref=src, dst_ref=dst, send_sem=sems[0].at[at], recv_sem=sems[1].at[at],
            device_id=to, device_id_type=MESH,
        ).start()

    def landed(block, sems, at):
        return pltpu.make_async_remote_copy(
            src_ref=block, dst_ref=block, send_sem=sems[0].at[at], recv_sem=sems[1].at[at],
            device_id=opposite, device_id_type=MESH,
        )

    go_sems, gf_sems = (go_send, go_recv), (gf_send, gf_recv)
    l_sems, rs_sems = (l_send, l_recv), (rs_send, rs_recv)

    pl.semaphore_wait(barrier, len(partners))
    for t in range(3):
        z_copy(t).start()
    for d in range(1, PLANE):
        send(gat_own.at[:, 0], gat_own.at[:, d], go_sems, 0, ahead[d])
    for o in range(1, 4):
        send(l_out.at[0], la_in.at[o], l_sems, 0, near[o])

    own_copy.wait()
    own_rows = own[...]
    own_keys = own_rows[:, 0, :]
    own_values = own_rows[:, 1, :]
    for k in range(KVH):
        own_k[k] = own_keys[:, k * DH : (k + 1) * DH]
        own_v[k] = own_values[:, k * DH : (k + 1) * DH]

    lane = lax.broadcasted_iota(jnp.int32, (1, PAIR), 1) % TOKENS
    weight = jnp.where(lane < length, adv_ref[0, 0], 0.0)
    key_at = lax.broadcasted_iota(jnp.int32, (TOKENS, PAIR), 0)
    query_at = lax.broadcasted_iota(jnp.int32, (TOKENS, PAIR), 1) % TOKENS
    causal = key_at <= query_at

    def pair_of(ref, k, c):
        return jnp.concatenate(
            [ref[k, :, (2 * c) * DH : (2 * c + 1) * DH], ref[k, :, (2 * c + 1) * DH : (2 * c + 2) * DH]], axis=0
        )

    def all_of(ref, k):
        return jnp.concatenate([ref[k, :, g * DH : (g + 1) * DH] for g in range(GQA)], axis=0)

    def rows_of(ref, k):
        tile = ref[k // 2].astype(F32)
        tile = jnp.where(k % 2 == 0, tile[:, 0:8, :], tile[:, 8:16, :])
        keys = [tile[s, 0:4] for s in range(PLANE)]
        values = [tile[s, 4:8] for s in range(PLANE)]
        return jnp.concatenate(keys, axis=0).astype(BF16), jnp.concatenate(values, axis=0).astype(BF16)

    def seen_part(k, rows, keys, values, mask, at):
        for c in range(GQA // 2):
            cols = slice(c * PAIR, (c + 1) * PAIR)
            score = dot_last(keys, pair_of(qs, k, c))
            if mask is not None:
                score = jnp.where(mask, score, LOW)
            peak = jnp.max(score, axis=0, keepdims=True)
            e = jnp.exp2((score - peak) * EXP_SCALE)
            dprob = dot_last(values, pair_of(dos, k, c))
            e_own[k, rows, cols] = e
            dp_own[k, rows, cols] = dprob
            stat[k, at : at + 1, cols] = peak
            stat[k, at + 1 : at + 2, cols] = jnp.sum(e, axis=0, keepdims=True)
            stat[k, at + 2 : at + 3, cols] = jnp.sum(e * dprob, axis=0, keepdims=True)

    def own_part(k):
        for copy in in_copies(k):
            copy.wait()
        seen_part(k, slice(0, TOKENS), own_k[k], own_v[k], causal, 0)

    def plane_part(k, carry):
        keys, values = rows_of(gat_own, k)
        pre_k[k, 0:HALF] = keys
        seen_part(k, slice(TOKENS, SEEN), keys, values, None, 5)
        return carry

    def own_parts(start, stop):
        def step(k, carry):
            own_part(k)
            return carry

        lax.fori_loop(start, stop, step, 0)

    def spread_own_all():
        return landed(gat_own.at[:, pl.ds(1, PLANE - 1)], go_sems, 0)

    def spread(t):
        z_copy(t).wait_recv()
        for d in range(1, PLANE):
            send(gat_far.at[t, 0], gat_far.at[t, d], gf_sems, t, ahead[d])

    def spread_all(t):
        return landed(gat_far.at[t, pl.ds(1, PLANE - 1)], gf_sems, t)

    own_parts(0, 1)
    landed(la_in.at[pl.ds(1, 3)], l_sems, 0).wait_recv()
    l_out[1] = l_out[0] + la_in[1] + la_in[2] + la_in[3]
    for o in range(1, 8):
        send(l_out.at[1], lb_in.at[o], l_sems, 1, far[o])
    own_parts(1, KVH)
    for t in range(3):
        spread(t)
    spread_own_all().wait_recv()
    lax.fori_loop(0, KVH, plane_part, 0)

    def scatter_all(k):
        return landed(rs_out.at[k, pl.ds(1, PLANE - 1)], rs_sems, k)

    def cross(k):
        return pltpu.make_async_remote_copy(
            src_ref=zs_out.at[k], dst_ref=zs_in.at[k], send_sem=zs_send.at[k], recv_sem=zs_recv.at[k],
            device_id=opposite, device_id_type=MESH,
        )

    def plane_sum(k):
        landed(rs_in.at[k, pl.ds(1, PLANE - 1)], rs_sems, k).wait_recv()
        total = part[k] + jnp.sum(rs_in[k, 1:PLANE].astype(F32), axis=0)
        part[k] = total
        zs_out[k] = total.astype(BF16)
        cross(k).start()

    def prefix_part(k, carry):
        @pl.when(k == 0)
        def _():
            spread_all(0).wait_recv()

        @pl.when(k == 2)
        def _():
            spread_all(1).wait_recv()

        @pl.when(k == 4)
        def _():
            spread_all(2).wait_recv()

        keys, values = rows_of(gat_far, k)
        pre_k[k, HALF:TOKENS] = keys
        for c in range(GQA // 2):
            cols = slice(c * PAIR, (c + 1) * PAIR)
            score = dot_last(keys, pair_of(qs, k, c))
            own_peak, near_peak = stat[k, 0:1, cols], stat[k, 5:6, cols]
            peak = jnp.maximum(jnp.maximum(own_peak, near_peak), jnp.max(score, axis=0, keepdims=True))
            e = jnp.exp2((score - peak) * EXP_SCALE)
            dprob = dot_last(values, pair_of(dos, k, c))
            shrink = jnp.exp2((own_peak - peak) * EXP_SCALE)
            near_shrink = jnp.exp2((near_peak - peak) * EXP_SCALE)
            total = shrink * stat[k, 1:2, cols] + near_shrink * stat[k, 6:7, cols]
            inverse = 1.0 / (jnp.sum(e, axis=0, keepdims=True) + total)
            products = shrink * stat[k, 2:3, cols] + near_shrink * stat[k, 7:8, cols]
            delta = (jnp.sum(e * dprob, axis=0, keepdims=True) + products) * inverse
            scaled = inverse * weight
            own_scaled = shrink * scaled
            near_prob = e_own[k, TOKENS:SEEN, cols] * (near_shrink * scaled)
            far_prob = e * scaled
            pt[0:HALF, cols] = near_prob.astype(BF16)
            pt[HALF:TOKENS, cols] = far_prob.astype(BF16)
            dst[k, 0:HALF, cols] = (near_prob * (dp_own[k, TOKENS:SEEN, cols] - delta)).astype(BF16)
            dst[k, HALF:TOKENS, cols] = (far_prob * (dprob - delta)).astype(BF16)
            stat[k, 3:4, cols] = own_scaled
            stat[k, 4:5, cols] = delta
        grad_k = dot(dst[k, 0:TOKENS, :], all_of(qs, k)) * FACTOR
        grad_v = dot(pt[...], all_of(dos, k))
        for d in range(PLANE):
            near_rows, far_rows = slice(4 * d, 4 * d + 4), slice(HALF + 4 * d, HALF + 4 * d + 4)
            tile = jnp.concatenate(
                [grad_k[near_rows], grad_k[far_rows], grad_v[near_rows], grad_v[far_rows]], axis=0
            )
            if d == 0:
                part[k] = tile
            else:
                rs_out[k, d] = tile.astype(BF16)
        for d in range(1, PLANE):
            send(rs_out.at[k, d], rs_in.at[k, d], rs_sems, k, behind[d])

        @pl.when(k == 1)
        def _():
            landed(lb_in.at[pl.ds(1, 7)], l_sems, 1).wait_recv()
            l_out[2] = l_out[1] + jnp.sum(lb_in[1:8], axis=0)
            for d in range(1, PLANE):
                send(l_out.at[2], lp_in.at[d], l_sems, 2, ahead[d])

        return carry

    lax.fori_loop(0, KVH, prefix_part, 0)

    def own_grads(k):
        for c in range(GQA // 2):
            cols = slice(c * PAIR, (c + 1) * PAIR)
            prob = e_own[k, 0:TOKENS, cols] * stat[k, 3:4, cols]
            pt[:, cols] = prob.astype(BF16)
            dst[k, TOKENS:PAIR, cols] = (prob * (dp_own[k, 0:TOKENS, cols] - stat[k, 4:5, cols])).astype(BF16)
        ogr[k, 0] = dot(dst[k, TOKENS:PAIR, :], all_of(qs, k)) * FACTOR
        ogr[k, 1] = dot(pt[...], all_of(dos, k))

    def own_grads_step(k, carry):
        own_grads(k)
        return carry

    def plane_sum_step(k, carry):
        plane_sum(k)
        return carry

    lax.fori_loop(0, 3, own_grads_step, 0)
    lax.fori_loop(0, 3, plane_sum_step, 0)
    lax.fori_loop(3, 4, own_grads_step, 0)
    lax.fori_loop(3, KVH, plane_sum_step, 0)
    lax.fori_loop(4, KVH, own_grads_step, 0)
    landed(lp_in.at[pl.ds(1, PLANE - 1)], l_sems, 2).wait_recv()
    scale = slots / (l_out[2] + jnp.sum(lp_in[1:PLANE], axis=0))
    scale_out[...] = scale
    one = scale[0:1, :]
    one_k = one * FACTOR

    def query_grads(k, carry):
        head = pl.ds(pl.multiple_of(k * DH, DH), DH)
        own_t[0, :, head] = (ogr[k, 0] * one).astype(BF16)
        own_t[1, :, head] = (ogr[k, 1] * one).astype(BF16)
        keys = jnp.concatenate([pre_k[k].astype(F32).T, own_k[k].astype(F32).T], axis=1).astype(BF16)
        for c in range(GQA // 2):
            turned = dot(keys, dst[k, :, c * PAIR : (c + 1) * PAIR])
            for g in range(2):
                at = pl.ds(pl.multiple_of(k * WIDTH + (2 * c + g) * DH, DH), DH)
                qg[:, at] = (turned[:, g * DH : (g + 1) * DH].T * one_k).astype(BF16)
        return carry

    lax.fori_loop(0, KVH, query_grads, 0)
    own_out[:, 0, :] = own_t[0]
    own_out[:, 1, :] = own_t[1]

    for k in range(KVH):
        cols = slice(k * DH, (k + 1) * DH)
        cross(k).wait_recv()
        there = zs_in[k].astype(F32)
        pre_out[:, 0, cols] = (part[k, 0:4] + there[4:8]) * one
        pre_out[:, 1, cols] = (part[k, 8:12] + there[12:16]) * one

    for k in range(KVH):
        scatter_all(k).wait_send()
        cross(k).wait_send()
    spread_own_all().wait_send()
    for t in range(3):
        spread_all(t).wait_send()
        z_copy(t).wait_send()
    landed(la_in.at[pl.ds(1, 3)], l_sems, 0).wait_send()
    landed(lb_in.at[pl.ds(1, 7)], l_sems, 1).wait_send()
    landed(lp_in.at[pl.ds(1, PLANE - 1)], l_sems, 2).wait_send()


def write_out(qg, own, pre, scale, qg_out, own_out, pre_out, scale_out, one, sems):
    one[...] = scale[0:1, 0:1]
    copies = [
        pltpu.make_async_copy(pre, pre_out, sems.at[0]),
        pltpu.make_async_copy(one, scale_out, sems.at[11]),
    ]
    for at in range(8):
        rows = pl.ds(16 * at, 16)
        copies.append(pltpu.make_async_copy(qg.at[rows], qg_out.at[rows], sems.at[1 + at]))
    for at in range(2):
        rows = pl.ds(64 * at, 64)
        copies.append(pltpu.make_async_copy(own.at[rows], own_out.at[rows], sems.at[9 + at]))
    for copy in copies:
        copy.start()
    for copy in copies:
        copy.wait()


def on_device(queries, own_kv, prefix_kv, out_grad, lengths, advantages):
    slots = float(
        queries.shape[2] * lax.axis_size("group") * lax.axis_size("resp") * lax.axis_size("vocab")
    )
    width = KVH * WIDTH
    vmem = pltpu.VMEM
    dma = pltpu.SemaphoreType.DMA
    in_hbm = pl.BlockSpec(memory_space=pltpu.HBM)
    in_smem = pl.BlockSpec(memory_space=pltpu.SMEM)
    in_vmem = pl.BlockSpec(memory_space=pltpu.VMEM)

    def body(*refs):
        kernel(slots, *refs)

    def held(x):
        return pltpu.with_memory_space_constraint(x, pltpu.HBM)

    query_shape, own_shape, prefix_shape = (TOKENS, width), (TOKENS, 2, KVH * DH), (4, 2, KVH * DH)
    query_grad, own_grad, prefix_grad, token_scale = pl.pallas_call(
        body,
        out_shape=(
            vmem(query_shape, BF16),
            vmem(own_shape, BF16),
            vmem(prefix_shape, F32),
            vmem((8, DH), F32),
        ),
        in_specs=[in_smem, in_smem, in_hbm, in_hbm, in_hbm, in_hbm],
        out_specs=(in_vmem, in_vmem, in_vmem, in_vmem),
        scratch_shapes=[
            vmem((KVH, TOKENS, WIDTH), BF16),
            vmem((KVH, TOKENS, WIDTH), BF16),
            vmem((TOKENS, 2, KVH * DH), BF16),
            vmem((4, 2, KVH * DH), BF16),
            vmem((KVH, TOKENS, DH), BF16),
            vmem((KVH, TOKENS, DH), BF16),
            vmem((KVH, TOKENS, DH), BF16),
            vmem((KVH, SEEN, WIDTH), F32),
            vmem((KVH, SEEN, WIDTH), F32),
            vmem((KVH, 8, WIDTH), F32),
            vmem((TOKENS, WIDTH), BF16),
            vmem((KVH, PAIR, WIDTH), BF16),
            vmem((KVH, 2, TOKENS, DH), F32),
            vmem((2, TOKENS, KVH * DH), BF16),
            vmem((3, PLANE, 16, DH), BF16),
            vmem((3, PLANE, 16, DH), BF16),
            vmem((KVH, PLANE, 16, DH), BF16),
            vmem((KVH, PLANE, 16, DH), BF16),
            vmem((KVH, 16, DH), F32),
            vmem((KVH, 16, DH), BF16),
            vmem((KVH, 16, DH), BF16),
            vmem((3, 8, DH), F32),
            vmem((4, 8, DH), F32),
            vmem((8, 8, DH), F32),
            vmem((PLANE, 8, DH), F32),
            dma((2, KVH)),
            dma((2,)),
            dma((3,)),
            dma((3,)),
            dma((1,)),
            dma((1,)),
            dma((3,)),
            dma((3,)),
            dma((KVH,)),
            dma((KVH,)),
            dma((KVH,)),
            dma((KVH,)),
            dma((3,)),
            dma((3,)),
        ],
        compiler_params=pltpu.CompilerParams(
            collective_id=0, has_side_effects=True, vmem_limit_bytes=48 * 1024 * 1024
        ),
        cost_estimate=pl.CostEstimate(
            flops=5 * KVH * 2 * WIDTH * PAIR * DH,
            bytes_accessed=5 * 1024 * 1024,
            transcendentals=KVH * WIDTH * PAIR,
        ),
    )(lengths, advantages, held(queries[0, 0]), held(own_kv[0, 0]), held(prefix_kv[0]), held(out_grad[0, 0]))
    query_grad, own_grad, prefix_grad, token_scale = pl.pallas_call(
        write_out,
        out_shape=(
            jax.ShapeDtypeStruct(query_shape, BF16),
            jax.ShapeDtypeStruct(own_shape, BF16),
            jax.ShapeDtypeStruct(prefix_shape, F32),
            jax.ShapeDtypeStruct((1, 1), F32),
        ),
        in_specs=[in_vmem] * 4,
        out_specs=(in_hbm,) * 4,
        scratch_shapes=[vmem((1, 1), F32), dma((12,))],
        compiler_params=pltpu.CompilerParams(vmem_limit_bytes=8 * 1024 * 1024),
    )(query_grad, own_grad, prefix_grad, token_scale)
    return query_grad[None, None], own_grad[None, None], prefix_grad[None], token_scale[0, 0]


def solution(mesh):
    in_specs = (
        P("group", ("resp", "vocab"), None, None),
        P("group", ("resp", "vocab"), None, None, None),
        P("group", ("resp", "vocab"), None, None),
        P("group", ("resp", "vocab"), None, None),
        P("group", ("resp", "vocab")),
        P("group", ("resp", "vocab")),
    )
    out_specs = (
        P("group", ("resp", "vocab"), None, None),
        P("group", ("resp", "vocab"), None, None, None),
        P("group", ("resp", "vocab"), None, None),
        P(),
    )
    return jax.shard_map(
        on_device, mesh=mesh, in_specs=in_specs, out_specs=out_specs, check_vma=False
    )
```

```python
import math

import jax
import jax.numpy as jnp
from jax import lax
from jax.experimental import pallas as pl
from jax.experimental.pallas import tpu as pltpu
from jax.sharding import PartitionSpec as P

DH = 128
KVH = 5
GQA = 8
TOKENS = 128
WIDTH = GQA * DH
PAIR = 2 * TOKENS
HALF = 64
SEEN = TOKENS + HALF
SIDE = 4
PLANE = SIDE * SIDE
FACTOR = 1.0 / math.sqrt(DH)
EXP_SCALE = FACTOR * math.log2(math.e)
LOW = -1e30
MESH = pl.DeviceIdType.MESH
F32 = jnp.float32
BF16 = jnp.bfloat16
LAST = (((1,), (1,)), ((), ()))


def dot_last(a, b):
    return lax.dot_general(a, b, LAST, preferred_element_type=F32)


def dot(a, b):
    return jnp.dot(a, b, preferred_element_type=F32)


def kernel(
    slots,
    len_ref, adv_ref, q_hbm, own_hbm, pre_hbm, do_hbm,
    qg, own_out, pre_out, scale_out,
    qs, dos, own, pre, own_k, own_v, pre_k, e_own, dp_own, stat, pt, dst, ogr, own_t,
    gat_own, gat_far, rs_out, rs_in, part, zs_out, zs_in, l_out, la_in, lb_in, lp_in,
    in_sem, small_sem, z_send, z_recv, go_send, go_recv, gf_send, gf_recv, rs_send, rs_recv, zs_send, zs_recv, l_send, l_recv,
):
    group = lax.axis_index("group")
    resp = lax.axis_index("resp")
    vocab = lax.axis_index("vocab")
    half = resp % 2
    row = resp // 2

    ahead, behind = [None], [None]
    for d in range(1, PLANE):
        down, over = d // SIDE, d % SIDE
        ahead.append((group, ((row + down) % SIDE) * 2 + half, (vocab + over) % SIDE))
        behind.append((group, ((row + SIDE - down) % SIDE) * 2 + half, (vocab + SIDE - over) % SIDE))
    opposite = (group, row * 2 + 1 - half, vocab)
    near = [None] + [((group // 4) * 4 + (group + o) % 4, resp, vocab) for o in range(1, 4)]
    far = [None] + [((group + 4 * o) % 16, resp, vocab) for o in range(1, 4)]
    far += [((group + 4 * o) % 16, row * 2 + 1 - half, vocab) for o in range(4)]

    barrier = pltpu.get_barrier_semaphore()
    partners = [opposite] + ahead[1:] + near[1:] + far[1:4] + far[5:]
    for partner in partners:
        pl.semaphore_signal(barrier, inc=1, device_id=partner, device_id_type=MESH)

    pre_copy = pltpu.make_async_copy(pre_hbm, pre, small_sem.at[0])
    own_copy = pltpu.make_async_copy(own_hbm, own, small_sem.at[1])
    pre_copy.start()
    own_copy.start()

    def in_copies(k):
        cols = pl.ds(pl.multiple_of(k * WIDTH, WIDTH), WIDTH)
        return (
            pltpu.make_async_copy(q_hbm.at[:, cols], qs.at[k], in_sem.at[0, k]),
            pltpu.make_async_copy(do_hbm.at[:, cols], dos.at[k], in_sem.at[1, k]),
        )

    for k in range(KVH):
        for copy in in_copies(k):
            copy.start()

    length = len_ref[0, 0]
    l_out[0] = jnp.full((8, DH), length.astype(F32))
    blank = jnp.zeros((8, DH), F32)
    pre_copy.wait()
    shard = pre[...].astype(F32)
    mine = []
    for k in range(KVH):
        cols = slice(k * DH, (k + 1) * DH)
        mine.append(jnp.concatenate([shard[:, 0, cols], shard[:, 1, cols]], axis=0))
    for t in range(3):
        low = mine[2 * t]
        high = mine[2 * t + 1] if 2 * t + 1 < KVH else blank
        gat_own[t, 0] = jnp.concatenate([low, high], axis=0).astype(BF16)

    def z_copy(t):
        return pltpu.make_async_remote_copy(
            src_ref=gat_own.at[t, 0], dst_ref=gat_far.at[t, 0], send_sem=z_send.at[t], recv_sem=z_recv.at[t],
            device_id=opposite, device_id_type=MESH,
        )

    def send(src, dst, sems, at, to):
        pltpu.make_async_remote_copy(
            src_ref=src, dst_ref=dst, send_sem=sems[0].at[at], recv_sem=sems[1].at[at],
            device_id=to, device_id_type=MESH,
        ).start()

    def landed(block, sems, at):
        return pltpu.make_async_remote_copy(
            src_ref=block, dst_ref=block, send_sem=sems[0].at[at], recv_sem=sems[1].at[at],
            device_id=opposite, device_id_type=MESH,
        )

    go_sems, gf_sems = (go_send, go_recv), (gf_send, gf_recv)
    l_sems, rs_sems = (l_send, l_recv), (rs_send, rs_recv)

    pl.semaphore_wait(barrier, len(partners))
    for t in range(3):
        z_copy(t).start()
    for d in range(1, PLANE):
        send(gat_own.at[:, 0], gat_own.at[:, d], go_sems, 0, ahead[d])
    for o in range(1, 4):
        send(l_out.at[0], la_in.at[o], l_sems, 0, near[o])

    own_copy.wait()
    own_rows = own[...]
    own_keys = own_rows[:, 0, :]
    own_values = own_rows[:, 1, :]
    for k in range(KVH):
        own_k[k] = own_keys[:, k * DH : (k + 1) * DH]
        own_v[k] = own_values[:, k * DH : (k + 1) * DH]

    lane = lax.broadcasted_iota(jnp.int32, (1, PAIR), 1) % TOKENS
    weight = jnp.where(lane < length, adv_ref[0, 0], 0.0)
    key_at = lax.broadcasted_iota(jnp.int32, (TOKENS, PAIR), 0)
    query_at = lax.broadcasted_iota(jnp.int32, (TOKENS, PAIR), 1) % TOKENS
    causal = key_at <= query_at

    def pair_of(ref, k, c):
        return jnp.concatenate(
            [ref[k, :, (2 * c) * DH : (2 * c + 1) * DH], ref[k, :, (2 * c + 1) * DH : (2 * c + 2) * DH]], axis=0
        )

    def all_of(ref, k):
        return jnp.concatenate([ref[k, :, g * DH : (g + 1) * DH] for g in range(GQA)], axis=0)

    def rows_of(ref, k):
        tile = ref[k // 2].astype(F32)
        tile = jnp.where(k % 2 == 0, tile[:, 0:8, :], tile[:, 8:16, :])
        keys = [tile[s, 0:4] for s in range(PLANE)]
        values = [tile[s, 4:8] for s in range(PLANE)]
        return jnp.concatenate(keys, axis=0).astype(BF16), jnp.concatenate(values, axis=0).astype(BF16)

    def seen_part(k, rows, keys, values, mask, at):
        for c in range(GQA // 2):
            cols = slice(c * PAIR, (c + 1) * PAIR)
            score = dot_last(keys, pair_of(qs, k, c))
            if mask is not None:
                score = jnp.where(mask, score, LOW)
            peak = jnp.max(score, axis=0, keepdims=True)
            e = jnp.exp2((score - peak) * EXP_SCALE)
            dprob = dot_last(values, pair_of(dos, k, c))
            e_own[k, rows, cols] = e
            dp_own[k, rows, cols] = dprob
            stat[k, at : at + 1, cols] = peak
            stat[k, at + 1 : at + 2, cols] = jnp.sum(e, axis=0, keepdims=True)
            stat[k, at + 2 : at + 3, cols] = jnp.sum(e * dprob, axis=0, keepdims=True)

    def own_part(k):
        for copy in in_copies(k):
            copy.wait()
        seen_part(k, slice(0, TOKENS), own_k[k], own_v[k], causal, 0)

    def plane_part(k, carry):
        keys, values = rows_of(gat_own, k)
        pre_k[k, 0:HALF] = keys
        seen_part(k, slice(TOKENS, SEEN), keys, values, None, 5)
        return carry

    def own_parts(start, stop):
        def step(k, carry):
            own_part(k)
            return carry

        lax.fori_loop(start, stop, step, 0)

    def spread_own_all():
        return landed(gat_own.at[:, pl.ds(1, PLANE - 1)], go_sems, 0)

    def spread(t):
        z_copy(t).wait_recv()
        for d in range(1, PLANE):
            send(gat_far.at[t, 0], gat_far.at[t, d], gf_sems, t, ahead[d])

    def spread_all(t):
        return landed(gat_far.at[t, pl.ds(1, PLANE - 1)], gf_sems, t)

    own_parts(0, 1)
    landed(la_in.at[pl.ds(1, 3)], l_sems, 0).wait_recv()
    l_out[1] = l_out[0] + la_in[1] + la_in[2] + la_in[3]
    for o in range(1, 8):
        send(l_out.at[1], lb_in.at[o], l_sems, 1, far[o])
    own_parts(1, 3)
    for t in range(3):
        spread(t)
    own_parts(3, KVH)
    spread_own_all().wait_recv()
    lax.fori_loop(0, KVH, plane_part, 0)

    def scatter_all(k):
        return landed(rs_out.at[k, pl.ds(1, PLANE - 1)], rs_sems, k)

    def cross(k):
        return pltpu.make_async_remote_copy(
            src_ref=zs_out.at[k], dst_ref=zs_in.at[k], send_sem=zs_send.at[k], recv_sem=zs_recv.at[k],
            device_id=opposite, device_id_type=MESH,
        )

    def plane_sum(k):
        landed(rs_in.at[k, pl.ds(1, PLANE - 1)], rs_sems, k).wait_recv()
        total = part[k] + jnp.sum(rs_in[k, 1:PLANE].astype(F32), axis=0)
        part[k] = total
        zs_out[k] = total.astype(BF16)
        cross(k).start()

    def prefix_part(k, carry):
        @pl.when(k == 0)
        def _():
            spread_all(0).wait_recv()

        @pl.when(k == 2)
        def _():
            spread_all(1).wait_recv()

        @pl.when(k == 4)
        def _():
            spread_all(2).wait_recv()

        keys, values = rows_of(gat_far, k)
        pre_k[k, HALF:TOKENS] = keys
        for c in range(GQA // 2):
            cols = slice(c * PAIR, (c + 1) * PAIR)
            score = dot_last(keys, pair_of(qs, k, c))
            own_peak, near_peak = stat[k, 0:1, cols], stat[k, 5:6, cols]
            peak = jnp.maximum(jnp.maximum(own_peak, near_peak), jnp.max(score, axis=0, keepdims=True))
            e = jnp.exp2((score - peak) * EXP_SCALE)
            dprob = dot_last(values, pair_of(dos, k, c))
            shrink = jnp.exp2((own_peak - peak) * EXP_SCALE)
            near_shrink = jnp.exp2((near_peak - peak) * EXP_SCALE)
            total = shrink * stat[k, 1:2, cols] + near_shrink * stat[k, 6:7, cols]
            inverse = 1.0 / (jnp.sum(e, axis=0, keepdims=True) + total)
            products = shrink * stat[k, 2:3, cols] + near_shrink * stat[k, 7:8, cols]
            delta = (jnp.sum(e * dprob, axis=0, keepdims=True) + products) * inverse
            scaled = inverse * weight
            own_scaled = shrink * scaled
            near_prob = e_own[k, TOKENS:SEEN, cols] * (near_shrink * scaled)
            far_prob = e * scaled
            pt[0:HALF, cols] = near_prob.astype(BF16)
            pt[HALF:TOKENS, cols] = far_prob.astype(BF16)
            dst[k, 0:HALF, cols] = (near_prob * (dp_own[k, TOKENS:SEEN, cols] - delta)).astype(BF16)
            dst[k, HALF:TOKENS, cols] = (far_prob * (dprob - delta)).astype(BF16)
            stat[k, 3:4, cols] = own_scaled
            stat[k, 4:5, cols] = delta
        grad_k = dot(dst[k, 0:TOKENS, :], all_of(qs, k)) * FACTOR
        grad_v = dot(pt[...], all_of(dos, k))
        for d in range(PLANE):
            near_rows, far_rows = slice(4 * d, 4 * d + 4), slice(HALF + 4 * d, HALF + 4 * d + 4)
            tile = jnp.concatenate(
                [grad_k[near_rows], grad_k[far_rows], grad_v[near_rows], grad_v[far_rows]], axis=0
            )
            if d == 0:
                part[k] = tile
            else:
                rs_out[k, d] = tile.astype(BF16)
        for d in range(1, PLANE):
            send(rs_out.at[k, d], rs_in.at[k, d], rs_sems, k, behind[d])

        @pl.when(k == 1)
        def _():
            landed(lb_in.at[pl.ds(1, 7)], l_sems, 1).wait_recv()
            l_out[2] = l_out[1] + jnp.sum(lb_in[1:8], axis=0)
            for d in range(1, PLANE):
                send(l_out.at[2], lp_in.at[d], l_sems, 2, ahead[d])

        return carry

    lax.fori_loop(0, KVH, prefix_part, 0)

    def own_grads(k):
        for c in range(GQA // 2):
            cols = slice(c * PAIR, (c + 1) * PAIR)
            prob = e_own[k, 0:TOKENS, cols] * stat[k, 3:4, cols]
            pt[:, cols] = prob.astype(BF16)
            dst[k, TOKENS:PAIR, cols] = (prob * (dp_own[k, 0:TOKENS, cols] - stat[k, 4:5, cols])).astype(BF16)
        ogr[k, 0] = dot(dst[k, TOKENS:PAIR, :], all_of(qs, k)) * FACTOR
        ogr[k, 1] = dot(pt[...], all_of(dos, k))

    def own_grads_step(k, carry):
        own_grads(k)
        return carry

    def plane_sum_step(k, carry):
        plane_sum(k)
        return carry

    lax.fori_loop(0, 3, own_grads_step, 0)
    lax.fori_loop(0, 3, plane_sum_step, 0)
    lax.fori_loop(3, 4, own_grads_step, 0)
    lax.fori_loop(3, KVH, plane_sum_step, 0)
    lax.fori_loop(4, KVH, own_grads_step, 0)
    landed(lp_in.at[pl.ds(1, PLANE - 1)], l_sems, 2).wait_recv()
    scale = slots / (l_out[2] + jnp.sum(lp_in[1:PLANE], axis=0))
    scale_out[...] = scale
    one = scale[0:1, :]
    one_k = one * FACTOR

    def query_grads(k, carry):
        head = pl.ds(pl.multiple_of(k * DH, DH), DH)
        own_t[0, :, head] = (ogr[k, 0] * one).astype(BF16)
        own_t[1, :, head] = (ogr[k, 1] * one).astype(BF16)
        keys = jnp.concatenate([pre_k[k].astype(F32).T, own_k[k].astype(F32).T], axis=1).astype(BF16)
        for c in range(GQA // 2):
            turned = dot(keys, dst[k, :, c * PAIR : (c + 1) * PAIR])
            for g in range(2):
                at = pl.ds(pl.multiple_of(k * WIDTH + (2 * c + g) * DH, DH), DH)
                qg[:, at] = (turned[:, g * DH : (g + 1) * DH].T * one_k).astype(BF16)
        return carry

    lax.fori_loop(0, KVH, query_grads, 0)
    own_out[:, 0, :] = own_t[0]
    own_out[:, 1, :] = own_t[1]

    for k in range(KVH):
        cols = slice(k * DH, (k + 1) * DH)
        cross(k).wait_recv()
        there = zs_in[k].astype(F32)
        pre_out[:, 0, cols] = (part[k, 0:4] + there[4:8]) * one
        pre_out[:, 1, cols] = (part[k, 8:12] + there[12:16]) * one

    for k in range(KVH):
        scatter_all(k).wait_send()
        cross(k).wait_send()
    spread_own_all().wait_send()
    for t in range(3):
        spread_all(t).wait_send()
        z_copy(t).wait_send()
    landed(la_in.at[pl.ds(1, 3)], l_sems, 0).wait_send()
    landed(lb_in.at[pl.ds(1, 7)], l_sems, 1).wait_send()
    landed(lp_in.at[pl.ds(1, PLANE - 1)], l_sems, 2).wait_send()


def write_out(qg, own, pre, scale, qg_out, own_out, pre_out, scale_out, one, sems):
    one[...] = scale[0:1, 0:1]
    copies = [
        pltpu.make_async_copy(pre, pre_out, sems.at[0]),
        pltpu.make_async_copy(one, scale_out, sems.at[11]),
    ]
    for at in range(8):
        rows = pl.ds(16 * at, 16)
        copies.append(pltpu.make_async_copy(qg.at[rows], qg_out.at[rows], sems.at[1 + at]))
    for at in range(2):
        rows = pl.ds(64 * at, 64)
        copies.append(pltpu.make_async_copy(own.at[rows], own_out.at[rows], sems.at[9 + at]))
    for copy in copies:
        copy.start()
    for copy in copies:
        copy.wait()


def on_device(queries, own_kv, prefix_kv, out_grad, lengths, advantages):
    slots = float(
        queries.shape[2] * lax.axis_size("group") * lax.axis_size("resp") * lax.axis_size("vocab")
    )
    width = KVH * WIDTH
    vmem = pltpu.VMEM
    dma = pltpu.SemaphoreType.DMA
    in_hbm = pl.BlockSpec(memory_space=pltpu.HBM)
    in_smem = pl.BlockSpec(memory_space=pltpu.SMEM)
    in_vmem = pl.BlockSpec(memory_space=pltpu.VMEM)

    def body(*refs):
        kernel(slots, *refs)

    def held(x):
        return pltpu.with_memory_space_constraint(x, pltpu.HBM)

    query_shape, own_shape, prefix_shape = (TOKENS, width), (TOKENS, 2, KVH * DH), (4, 2, KVH * DH)
    query_grad, own_grad, prefix_grad, token_scale = pl.pallas_call(
        body,
        out_shape=(
            vmem(query_shape, BF16),
            vmem(own_shape, BF16),
            vmem(prefix_shape, F32),
            vmem((8, DH), F32),
        ),
        in_specs=[in_smem, in_smem, in_hbm, in_hbm, in_hbm, in_hbm],
        out_specs=(in_vmem, in_vmem, in_vmem, in_vmem),
        scratch_shapes=[
            vmem((KVH, TOKENS, WIDTH), BF16),
            vmem((KVH, TOKENS, WIDTH), BF16),
            vmem((TOKENS, 2, KVH * DH), BF16),
            vmem((4, 2, KVH * DH), BF16),
            vmem((KVH, TOKENS, DH), BF16),
            vmem((KVH, TOKENS, DH), BF16),
            vmem((KVH, TOKENS, DH), BF16),
            vmem((KVH, SEEN, WIDTH), F32),
            vmem((KVH, SEEN, WIDTH), F32),
            vmem((KVH, 8, WIDTH), F32),
            vmem((TOKENS, WIDTH), BF16),
            vmem((KVH, PAIR, WIDTH), BF16),
            vmem((KVH, 2, TOKENS, DH), F32),
            vmem((2, TOKENS, KVH * DH), BF16),
            vmem((3, PLANE, 16, DH), BF16),
            vmem((3, PLANE, 16, DH), BF16),
            vmem((KVH, PLANE, 16, DH), BF16),
            vmem((KVH, PLANE, 16, DH), BF16),
            vmem((KVH, 16, DH), F32),
            vmem((KVH, 16, DH), BF16),
            vmem((KVH, 16, DH), BF16),
            vmem((3, 8, DH), F32),
            vmem((4, 8, DH), F32),
            vmem((8, 8, DH), F32),
            vmem((PLANE, 8, DH), F32),
            dma((2, KVH)),
            dma((2,)),
            dma((3,)),
            dma((3,)),
            dma((1,)),
            dma((1,)),
            dma((3,)),
            dma((3,)),
            dma((KVH,)),
            dma((KVH,)),
            dma((KVH,)),
            dma((KVH,)),
            dma((3,)),
            dma((3,)),
        ],
        compiler_params=pltpu.CompilerParams(
            collective_id=0, has_side_effects=True, vmem_limit_bytes=48 * 1024 * 1024
        ),
        cost_estimate=pl.CostEstimate(
            flops=5 * KVH * 2 * WIDTH * PAIR * DH,
            bytes_accessed=5 * 1024 * 1024,
            transcendentals=KVH * WIDTH * PAIR,
        ),
    )(lengths, advantages, held(queries[0, 0]), held(own_kv[0, 0]), held(prefix_kv[0]), held(out_grad[0, 0]))
    query_grad, own_grad, prefix_grad, token_scale = pl.pallas_call(
        write_out,
        out_shape=(
            jax.ShapeDtypeStruct(query_shape, BF16),
            jax.ShapeDtypeStruct(own_shape, BF16),
            jax.ShapeDtypeStruct(prefix_shape, F32),
            jax.ShapeDtypeStruct((1, 1), F32),
        ),
        in_specs=[in_vmem] * 4,
        out_specs=(in_hbm,) * 4,
        scratch_shapes=[vmem((1, 1), F32), dma((12,))],
        compiler_params=pltpu.CompilerParams(vmem_limit_bytes=8 * 1024 * 1024),
    )(query_grad, own_grad, prefix_grad, token_scale)
    return query_grad[None, None], own_grad[None, None], prefix_grad[None], token_scale[0, 0]


def solution(mesh):
    in_specs = (
        P("group", ("resp", "vocab"), None, None),
        P("group", ("resp", "vocab"), None, None, None),
        P("group", ("resp", "vocab"), None, None),
        P("group", ("resp", "vocab"), None, None),
        P("group", ("resp", "vocab")),
        P("group", ("resp", "vocab")),
    )
    out_specs = (
        P("group", ("resp", "vocab"), None, None),
        P("group", ("resp", "vocab"), None, None, None),
        P("group", ("resp", "vocab"), None, None),
        P(),
    )
    return jax.shard_map(
        on_device, mesh=mesh, in_specs=in_specs, out_specs=out_specs, check_vma=False
    )
```
